32 devices in a mesh: space: 4 (over y, core), band: 8 (over z, x).
Axes of the slice: x: 2, y: 2, z: 4, core: 2. Of those that a mesh axis runs over, the one named last changes fastest.
Arguments:
- orbitals: float32 [64, 48, 16, 128], P('band', 'space'), may hold values from -12 to 12
- potential: float32 [48, 16, 128], P('space'), may hold values from -2 to 2
Outputs:
- filtered: float32 [64, 48, 16, 128], P('band', 'space')
- intersection: float32 [64, 64], P('band')
- projected: float32 [64, 64], P('band')
The draws below stay inside these ranges and needn't reach their ends.
All inputs are finite; a program needn't handle non-finite values.
Results may differ from the reference program's by a relative error of at most 0.0003.
Values may be sent and summed in bfloat16 or wider, within the bound.
No kernel may reach another device: no remote copies, remote signals or barrier semaphores. Data moves between devices by JAX's collectives and lax.ppermute only.
A program may use at most 128 MiB of HBM per device.

```python
import math
import jax
import jax.numpy as jnp
from jax import lax

ORBITALS = 64
NX = 16
NY = 128
NZ = 48


def draw_orbitals(key, part):
    keys = jax.random.split(key, 6)
    base = jnp.clip(jax.random.normal(keys[0], (ORBITALS, NZ, NX, NY), jnp.float32), -4.0, 4.0)
    common = jnp.clip(jax.random.normal(keys[1], (NZ, NX, NY), jnp.float32), -4.0, 4.0)
    zpos = jnp.arange(NZ, dtype=jnp.float32) / (NZ - 1)
    weights = jax.random.uniform(keys[2], (ORBITALS,), jnp.float32, 0.3, 1.0)
    wave_weights = jax.random.uniform(keys[5], (ORBITALS,), jnp.float32, 0.6, 1.0)
    ramp = 1.0 + zpos
    phases = jax.random.uniform(keys[4], (3, ORBITALS), jnp.float32, 0.0, 2.0 * math.pi)
    quarter = 0.5 * math.pi
    zcell = jnp.arange(NZ, dtype=jnp.float32)
    xcell = jnp.arange(NX, dtype=jnp.float32)
    ycell = jnp.arange(NY, dtype=jnp.float32)
    wave_z = jnp.cos(quarter * zcell[None, :] + phases[0][:, None])
    wave_x = jnp.cos(quarter * xcell[None, :] + phases[1][:, None])
    wave_y = jnp.cos(quarter * ycell[None, :] + phases[2][:, None])
    waves = wave_z[:, :, None, None] + wave_x[:, None, :, None] + wave_y[:, None, None, :]
    waves = 2.0 * wave_weights[:, None, None, None] * waves
    shared = ramp[:, None, None] * common
    values = base + weights[:, None, None, None] * shared[None] + waves
    return jnp.clip(values, -12.0, 12.0)


def shard_levels(own_key, extent, cuts, smallest, high):
    gain = 1.0
    for dim, blocks in cuts:
        steps = jax.random.uniform(jax.random.fold_in(jax.random.fold_in(own_key, 6), dim), (blocks,), jnp.float32, smallest / len(cuts), high / len(cuts))
        gain = gain * jnp.repeat(jnp.exp(steps), extent[dim] // blocks).reshape((-1,) + (1,) * (len(extent) - 1 - dim))
    return gain


def setup_inputs(seed: int = 0) -> dict:
    splits = jax.random.split(jax.random.key(seed), 3)
    return {
        "orbitals": draw_orbitals(jax.random.fold_in(splits[2], 71), 0),
        "potential": jnp.clip(jax.random.uniform(splits[1], (NZ, NX, NY), jnp.float32, -2.0, 2.0) * shard_levels(splits[1], (NZ, NX, NY), ((0, 4),), -0.4, 0.0), -2.0, 2.0),
    }


STENCIL = (-5369.0 / 1800.0, 12.0 / 7.0, -15.0 / 56.0, 10.0 / 189.0, -1.0 / 112.0, 2.0 / 1925.0, -1.0 / 16632.0)


def laplace(field):
    summed = 3.0 * STENCIL[0] * field
    for offset in range(1, 7):
        factor = STENCIL[offset]
        for axis_id in range(3):
            summed = summed + factor * (jnp.roll(field, offset, axis_id) + jnp.roll(field, -offset, axis_id))
    return summed


def hamiltonian(field, potential):
    return -0.5 * laplace(field) + potential * field


def filter_step(field, potential):
    return (hamiltonian(field, potential) - 9.0 * field) * 0.125


def reference(orbitals, potential):
    def single(field):
        first = filter_step(field, potential)
        second = 2.0 * filter_step(first, potential) - field
        applied = hamiltonian(second, potential).astype(jnp.bfloat16)
        return second, applied

    filtered, applied = lax.map(single, orbitals)
    inverse = 1.0 / (NZ * NX * NY)
    narrow = filtered.astype(jnp.bfloat16).reshape(ORBITALS, -1)
    narrow_applied = applied.reshape(ORBITALS, -1)
    intersection = jnp.dot(narrow, narrow.T, preferred_element_type=jnp.float32) * inverse
    projected = jnp.dot(narrow_applied, narrow.T, preferred_element_type=jnp.float32) * inverse
    return filtered, intersection, projected
```

```python
import functools

import jax
import jax.numpy as jnp
from jax import lax
from jax.experimental import pallas as pl
from jax.experimental.pallas import tpu as pltpu
from jax.sharding import PartitionSpec as P

STENCIL = (
    -5369.0 / 1800.0,
    12.0 / 7.0,
    -15.0 / 56.0,
    10.0 / 189.0,
    -1.0 / 112.0,
    2.0 / 1925.0,
    -1.0 / 16632.0,
)
WIDTH = 6
BF16 = jnp.bfloat16
F32 = jnp.float32
VMEM = pl.BlockSpec(memory_space=pltpu.VMEM)
PARAMS = pltpu.CompilerParams(vmem_limit_bytes=40 * 1024 * 1024)

GROUP = 8


def apply_row(load, center, where, nx, plane_rows, factors, diagonal):
    results = []
    for x in range(nx):
        here = center[x]
        total = diagonal(x) * here
        for k in range(1, WIDTH + 1):
            near = load(where + k * plane_rows + x * GROUP) + load(where - k * plane_rows + x * GROUP)
            near = near + (center[(x + k) % nx] + center[(x - k) % nx])
            near = near + (pltpu.roll(here, k, 1) + pltpu.roll(here, here.shape[1] - k, 1))
            total = total + factors[k - 1] * near
        results.append(total)
    return results


def loader(ref):
    def load(row):
        return ref[pl.ds(pl.multiple_of(row, GROUP), GROUP), :]

    return load


L_FACTORS = tuple(-0.0625 * c for c in STENCIL[1:])
L_CENTER = (-1.5 * STENCIL[0] - 9.0) / 8.0
H_FACTORS = tuple(-0.5 * c for c in STENCIL[1:])
H_CENTER = -1.5 * STENCIL[0]


def prepare_kernel(planes, nx, orbitals_ref, potential_ref, own_ref, left_ref, right_ref):
    rows = planes * nx
    plane_rows = nx * GROUP

    @pl.loop(0, rows // 2, unroll=8)
    def _(pair):
        row = pair * 2
        both = jnp.concatenate(
            [
                orbitals_ref[pl.ds(row, GROUP, stride=rows), :],
                orbitals_ref[pl.ds(row + 1, GROUP, stride=rows), :],
            ],
            axis=0,
        )
        at = pl.ds(pl.multiple_of(row * GROUP, 2 * GROUP), 2 * GROUP)
        own_ref[at, :] = both
        high = both.astype(BF16)
        left_ref[at, :] = high
        right_ref[at, :] = high

    extra = planes * plane_rows
    for out_ref, plane in ((left_ref, 0), (right_ref, planes - 1)):
        for x in range(0, nx, 2):
            block = own_ref[pl.ds(plane * plane_rows + x * GROUP, 2 * GROUP), :]
            low = block - block.astype(BF16).astype(F32)
            out_ref[pl.ds(extra + x * GROUP, 2 * GROUP), :] = low.astype(BF16)
    extra += plane_rows
    for out_ref, first, nearest in ((left_ref, 0, 0), (right_ref, planes - WIDTH, planes - 2)):
        for i in range(WIDTH):
            block = potential_ref[pl.ds((first + i) * nx, nx), :]
            out_ref[pl.ds(extra + i * nx, nx), :] = block.astype(BF16)
        for i in range(2):
            block = potential_ref[pl.ds((nearest + i) * nx, nx), :]
            low = block - block.astype(BF16).astype(F32)
            out_ref[pl.ds(extra + (WIDTH + i) * nx, nx), :] = low.astype(BF16)


def two_steps_kernel(
    planes, nx, own_ref, potential_ref, from_left_ref, from_right_ref,
    second_ref, filtered_ref, to_left_ref, to_right_ref, field, first, levels,
):
    plane_rows = nx * GROUP
    rows = planes * nx
    size = planes * plane_rows
    field[pl.ds(size, size), :] = own_ref[...]
    field[pl.ds(0, size), :] = from_left_ref[pl.ds(0, size), :].astype(F32)
    field[pl.ds(2 * size, size), :] = from_right_ref[pl.ds(0, size), :].astype(F32)
    for plane, ref in ((planes - 1, from_left_ref), (2 * planes, from_right_ref)):
        at = pl.ds(plane * plane_rows, plane_rows)
        field[at, :] = field[at, :] + ref[pl.ds(size, plane_rows), :].astype(F32)
    extra = size + plane_rows
    side = WIDTH * nx
    levels[pl.ds(side, rows), :] = potential_ref[...]
    for plane, nearest, ref in ((0, WIDTH - 2, from_left_ref), (WIDTH + planes, WIDTH + planes, from_right_ref)):
        levels[pl.ds(plane * nx, side), :] = ref[pl.ds(extra, side), :].astype(F32)
        at = pl.ds(nearest * nx, 2 * nx)
        levels[at, :] = levels[at, :] + ref[pl.ds(extra + side, 2 * nx), :].astype(F32)

    def diagonal(plane):
        def at(x):
            row = levels[pl.ds(plane * nx + x, 1), :]
            return jnp.broadcast_to(0.125 * row + L_CENTER, (GROUP, row.shape[1]))

        return at

    load = loader(field)

    @pl.loop(0, planes + 2 * WIDTH)
    def _(plane):
        where = (plane + planes - WIDTH) * plane_rows
        center = [load(where + x * GROUP) for x in range(nx)]
        total = apply_row(load, center, where, nx, plane_rows, L_FACTORS, diagonal(plane))
        for x in range(nx):
            first[pl.ds(pl.multiple_of(plane * plane_rows + x * GROUP, GROUP), GROUP), :] = total[x]

    load_first = loader(first)

    def second_step(plane, halo_ref, halo_plane):
        where = (plane + WIDTH) * plane_rows
        center = [load_first(where + x * GROUP) for x in range(nx)]
        total = apply_row(load_first, center, where, nx, plane_rows, L_FACTORS, diagonal(plane + WIDTH))
        base = plane * plane_rows
        values = []
        for x in range(nx):
            value = 2.0 * total[x] - load(size + base + x * GROUP)
            second_ref[pl.ds(pl.multiple_of(base + x * GROUP, GROUP), GROUP), :] = value
            filtered_ref[pl.ds(plane * nx + x, GROUP, stride=rows), :] = value
            values.append(value)
        for x in range(0, nx, 2):
            at = pl.ds(pl.multiple_of(halo_plane * plane_rows + x * GROUP, 2 * GROUP), 2 * GROUP)
            halo_ref[at, :] = jnp.concatenate(values[x : x + 2], axis=0).astype(BF16)

    @pl.loop(0, WIDTH)
    def _(plane):
        second_step(plane, to_left_ref, plane)

    @pl.loop(0, WIDTH)
    def _(plane):
        second_step(plane + planes - WIDTH, to_right_ref, plane)


def applied_kernel(planes, nx, second_ref, potential_ref, from_left_ref, from_right_ref, out_ref, field):
    plane_rows = nx * GROUP
    size = planes * plane_rows
    side = WIDTH * plane_rows
    field[pl.ds(side, size), :] = second_ref[...]
    field[pl.ds(0, side), :] = from_left_ref[...].astype(F32)
    field[pl.ds(side + size, side), :] = from_right_ref[...].astype(F32)
    load = loader(field)

    @pl.loop(0, planes)
    def _(plane):
        where = (plane + WIDTH) * plane_rows

        def diagonal(x):
            row = potential_ref[pl.ds(plane * nx + x, 1), :]
            return jnp.broadcast_to(row + H_CENTER, (GROUP, row.shape[1]))

        center = [load(where + x * GROUP) for x in range(nx)]
        total = apply_row(load, center, where, nx, plane_rows, H_FACTORS, diagonal)
        for x in range(nx):
            at = pl.multiple_of((plane * nx + x) * 2 * GROUP, 2 * GROUP)
            out_ref[pl.ds(at, 2 * GROUP), :] = jnp.concatenate([center[x], total[x]], axis=0).astype(BF16)


def gram_kernel(band, space, steps, in_ref, out_ref):
    width = 2 * GROUP
    total = jnp.zeros((band * width, band * width), F32)
    for step in range(0, steps, 2):
        block = jnp.concatenate(
            [in_ref[:, pl.ds((step + i) * width, width), :].reshape(band * width, -1) for i in range(2)],
            axis=1,
        )
        total = total + lax.dot_general(
            block, block, (((1,), (1,)), ((), ())), preferred_element_type=F32
        )
    lanes = lax.broadcasted_iota(jnp.int32, (GROUP, band * width), 1)
    for b in range(band):
        narrow = total[b * width : b * width + GROUP]
        applied = pltpu.roll(total[b * width + GROUP : (b + 1) * width], GROUP, 1)
        piece = jnp.where(lanes % width < GROUP, narrow, applied)
        for s in range(space):
            out_ref[s * band + b] = piece


def sum_kernel(scale, in_ref, intersection_ref, projected_ref):
    total = in_ref[0]
    for i in range(1, in_ref.shape[0]):
        total = total + in_ref[i]
    total = total * scale
    lanes, columns = total.shape[1], intersection_ref.shape[1]
    source = lax.broadcasted_iota(jnp.int32, (lanes, columns), 0)
    target = lax.broadcasted_iota(jnp.int32, (lanes, columns), 1)
    place = (target // GROUP) * (2 * GROUP) + target % GROUP
    for offset, ref in ((0, intersection_ref), (GROUP, projected_ref)):
        pick = jnp.where(source == place + offset, 1.0, 0.0).astype(F32)
        ref[...] = jnp.dot(total, pick, precision=lax.Precision.HIGHEST, preferred_element_type=F32)


def call(kernel, outs, *args, scratch=(), flops=1000000):
    return pl.pallas_call(
        kernel,
        out_shape=outs,
        in_specs=[VMEM] * len(args),
        out_specs=jax.tree.map(lambda _: VMEM, outs),
        scratch_shapes=list(scratch),
        compiler_params=PARAMS,
        cost_estimate=pl.CostEstimate(flops=flops, bytes_accessed=1000000, transcendentals=0),
    )(*args)


def shifts(axis):
    count = lax.axis_size(axis)
    up = [(i, (i + 1) % count) for i in range(count)]
    return up, [(j, i) for i, j in up]


def local_kernels(orbitals, potential):
    count, planes, nx, ny = orbitals.shape
    space, band = lax.axis_size("space"), lax.axis_size("band")
    rows = planes * nx
    plane_rows = nx * GROUP
    size = planes * plane_rows
    struct = jax.ShapeDtypeStruct
    levels = potential.reshape(rows, ny)
    up, down = shifts("space")

    message = struct((size + 2 * plane_rows, ny), BF16)
    own, to_left, to_right = call(
        functools.partial(prepare_kernel, planes, nx),
        (struct((size, ny), F32), message, message),
        orbitals.reshape(count * rows, ny), levels,
    )
    from_left = lax.ppermute(to_right, "space", up)
    from_right = lax.ppermute(to_left, "space", down)
    halo = struct((WIDTH * plane_rows, ny), BF16)
    second, filtered, to_left, to_right = call(
        functools.partial(two_steps_kernel, planes, nx),
        (struct((size, ny), F32), struct((count * rows, ny), F32), halo, halo),
        own, levels, from_left, from_right,
        scratch=[
            pltpu.VMEM((3 * size, ny), F32),
            pltpu.VMEM(((planes + 2 * WIDTH) * plane_rows, ny), F32),
            pltpu.VMEM(((planes + 2 * WIDTH) * nx, ny), F32),
        ],
    )
    from_left = lax.ppermute(to_right, "space", up)
    from_right = lax.ppermute(to_left, "space", down)
    pairs = call(
        functools.partial(applied_kernel, planes, nx),
        struct((rows * 2 * GROUP, ny), BF16),
        second, levels, from_left, from_right,
        scratch=[pltpu.VMEM(((planes + 2 * WIDTH) * plane_rows, ny), F32)],
    )
    steps = rows // band
    pairs = lax.all_to_all(pairs.reshape(band, steps * 2 * GROUP, ny), "band", 0, 0, tiled=True)
    pieces = call(
        functools.partial(gram_kernel, band, space, steps),
        struct((space * band, GROUP, band * 2 * GROUP), F32),
        pairs,
    )
    pieces = lax.all_to_all(pieces, ("space", "band"), 0, 0, tiled=True)
    total = count * band
    rows_out = struct((count, total), F32)
    intersection, projected = call(
        functools.partial(sum_kernel, 1.0 / (rows * ny * space)), (rows_out, rows_out), pieces
    )
    return filtered.reshape(orbitals.shape), intersection, projected


def padded(cells, width):
    up, down = shifts("space")
    head, tail = cells[:, :width], cells[:, cells.shape[1] - width :]
    return jnp.concatenate(
        [lax.ppermute(tail, "space", up), cells, lax.ppermute(head, "space", down)], axis=1
    )


def hamiltonian(beside, potential):
    planes = beside.shape[1] - 2 * WIDTH
    center = beside[:, WIDTH : WIDTH + planes]
    summed = 3.0 * STENCIL[0] * center
    for k in range(1, WIDTH + 1):
        near = beside[:, WIDTH + k : WIDTH + k + planes] + beside[:, WIDTH - k : WIDTH - k + planes]
        for dim in (2, 3):
            near = near + (jnp.roll(center, k, dim) + jnp.roll(center, -k, dim))
        summed = summed + STENCIL[k] * near
    return -0.5 * summed + potential * center


def local_plain(orbitals, potential):
    def step(field):
        return (hamiltonian(padded(field, WIDTH), potential) - 9.0 * field) * 0.125

    filtered = 2.0 * step(step(orbitals)) - orbitals
    beside = padded(filtered.astype(BF16), WIDTH).astype(F32)
    applied = hamiltonian(beside, potential).astype(BF16)
    count = orbitals.shape[0]
    narrow = filtered.astype(BF16).reshape(count, -1)
    applied = applied.reshape(count, -1)
    everyone = lax.all_gather(narrow, "band", axis=0, tiled=True)
    contract = (((1,), (1,)), ((), ()))
    parts = [
        lax.dot_general(rows, everyone, contract, preferred_element_type=F32)
        for rows in (narrow, applied)
    ]
    scale = 1.0 / (narrow.shape[1] * lax.axis_size("space"))
    intersection, projected = lax.psum(tuple(parts), "space")
    return filtered, intersection * scale, projected * scale


def local(orbitals, potential):
    count, planes, nx, ny = orbitals.shape
    band = lax.axis_size("band")
    fits = (
        count == GROUP
        and planes >= 2 * WIDTH
        and nx == 16
        and ny == 128
        and band * 2 * GROUP == 128
        and (planes * nx) % (2 * band) == 0
    )
    return (local_kernels if fits else local_plain)(orbitals, potential)


def solution(mesh):
    return jax.shard_map(
        local,
        mesh=mesh,
        in_specs=(P("band", "space", None, None), P("space", None, None)),
        out_specs=(P("band", "space", None, None), P("band", None), P("band", None)),
        check_vma=False,
    )
```

```python
import functools

import jax
import jax.numpy as jnp
from jax import lax
from jax.experimental import pallas as pl
from jax.experimental.pallas import tpu as pltpu
from jax.sharding import PartitionSpec as P

STENCIL = (
    -5369.0 / 1800.0,
    12.0 / 7.0,
    -15.0 / 56.0,
    10.0 / 189.0,
    -1.0 / 112.0,
    2.0 / 1925.0,
    -1.0 / 16632.0,
)
WIDTH = 6
BF16 = jnp.bfloat16
F32 = jnp.float32
VMEM = pl.BlockSpec(memory_space=pltpu.VMEM)
PARAMS = pltpu.CompilerParams(vmem_limit_bytes=40 * 1024 * 1024)

GROUP = 8

H_FACTORS = tuple(-0.5 * c for c in STENCIL[1:])
H_CENTER = -1.5 * STENCIL[0]
L_FACTORS = tuple(0.125 * c for c in H_FACTORS)
L_CENTER = (H_CENTER - 9.0) / 8.0


def aligned(start, size):
    return pl.ds(pl.multiple_of(start, size), size)


def low_part(block):
    return block - block.astype(BF16).astype(F32)


def circulant(ny):
    row = lax.broadcasted_iota(jnp.int32, (ny, ny), 0)
    column = lax.broadcasted_iota(jnp.int32, (ny, ny), 1)
    apart = jnp.abs(row - column)
    apart = jnp.minimum(apart, ny - apart)
    matrix = jnp.zeros((ny, ny), F32)
    for k in range(1, WIDTH + 1):
        matrix = jnp.where(apart == k, H_FACTORS[k - 1], matrix)
    high = matrix.astype(BF16)
    return jnp.concatenate([high, low_part(matrix).astype(BF16), high], axis=0)


def along_y(matrix, source, start, count, y_ref, plane_rows):
    step = min(count, WIDTH)
    for i in range(0, count, step):
        block = source[pl.ds((start + i) * plane_rows, step * plane_rows), :]
        high = block.astype(BF16)
        parts = jnp.concatenate([high, high, low_part(block).astype(BF16)], axis=1)
        y_ref[pl.ds(i * plane_rows, step * plane_rows), :] = jnp.dot(
            parts, matrix, preferred_element_type=F32
        )


def apply_planes(matrix, source, start, count, nx, y_ref, levels, level, linear, emit):
    plane_rows = nx * GROUP
    along_y(matrix, source, start, count, y_ref, plane_rows)
    factors, scale = (L_FACTORS, 0.125) if linear else (H_FACTORS, 1.0)

    def load(row):
        return source[aligned(row, GROUP), :]

    @pl.loop(0, count)
    def _(i):
        where = (start + i) * plane_rows
        center = [load(where + x * GROUP) for x in range(nx)]
        values = []
        for x in range(nx):
            row = levels[pl.ds((level + i) * nx + x, 1), :]
            row = 0.125 * row + L_CENTER if linear else row + H_CENTER
            total = jnp.broadcast_to(row, center[x].shape) * center[x]
            total = total + scale * y_ref[aligned(i * plane_rows + x * GROUP, GROUP), :]
            for k in range(1, WIDTH + 1):
                near = load(where + k * plane_rows + x * GROUP) + load(where - k * plane_rows + x * GROUP)
                near = near + (center[(x + k) % nx] + center[(x - k) % nx])
                total = total + factors[k - 1] * near
            values.append(total)
        emit(i, values, center)


def prepare_kernel(
    planes, nx, orbitals_hbm, potential_hbm, own_ref, level_ref, chip_ref, core_ref,
    orbitals, potential, semaphores,
):
    plane_rows = nx * GROUP
    rows = planes * nx
    parts = semaphores.shape[0] - 1
    each = planes // parts
    odd = lax.rem(lax.axis_index("space"), 2)

    def fetch(i):
        at = pl.ds(i * each, each)
        return pltpu.make_async_copy(orbitals_hbm.at[:, at], orbitals.at[:, at], semaphores.at[i])

    fetch_levels = pltpu.make_async_copy(potential_hbm, potential, semaphores.at[parts])
    for i in range(parts):
        fetch(i).start()
    fetch_levels.start()
    cells = orbitals.reshape(GROUP * rows, orbitals.shape[-1])
    for i in range(parts):
        fetch(i).wait()

        @pl.loop(i * each, (i + 1) * each)
        def _(plane):
            target = lax.select(odd == 1, planes - 1 - plane, plane) * plane_rows
            for x in range(0, nx, 2):
                row = plane * nx + x
                both = jnp.concatenate(
                    [cells[pl.ds(row + j, GROUP, stride=rows), :] for j in range(2)], axis=0
                )
                at = aligned(target + x * GROUP, 2 * GROUP)
                own_ref[at, :] = both
                high = both.astype(BF16)
                chip_ref[at, :] = high
                core_ref[at, :] = high

    fetch_levels.wait()
    extra = planes * plane_rows
    for out_ref, plane in ((chip_ref, 0), (core_ref, planes - 1)):
        block = own_ref[pl.ds(plane * plane_rows, plane_rows), :]
        out_ref[pl.ds(extra, plane_rows), :] = low_part(block).astype(BF16)
    extra += plane_rows
    for plane in range(planes):
        source = lax.select(odd == 1, planes - 1 - plane, plane) * nx
        block = potential[aligned(source, nx), :]
        level_ref[pl.ds(plane * nx, nx), :] = block
        for out_ref, first in ((chip_ref, 0), (core_ref, planes - NEAR)):
            out_ref[pl.ds(extra + plane * nx, nx), :] = block.astype(BF16)
            if first <= plane < first + NEAR:
                at = extra + (planes + plane - first) * nx
                out_ref[pl.ds(at, nx), :] = low_part(block).astype(BF16)


NEAR = 4


def place_planes(message, count, field, where, step, plane_rows):
    for i in range(count):
        block = message[pl.ds(i * plane_rows, plane_rows), :]
        field[pl.ds((where + step * i) * plane_rows, plane_rows), :] = block.astype(F32)


def add_low(message, planes, field, where, plane_rows):
    at = pl.ds(where * plane_rows, plane_rows)
    field[at, :] = field[at, :] + message[pl.ds(planes * plane_rows, plane_rows), :].astype(F32)


def place_levels(message, planes, nx, levels, where, step, near):
    extra = (planes + 1) * nx * GROUP
    for i in range(planes):
        block = message[pl.ds(extra + i * nx, nx), :].astype(F32)
        if near <= i < near + NEAR:
            block = block + message[pl.ds(extra + (planes + i - near) * nx, nx), :].astype(F32)
        levels[pl.ds((where + step * i) * nx, nx), :] = block


def store_planes(ref, first, nx):
    def emit(i, values, center):
        for x in range(nx):
            ref[aligned(((first + i) * nx + x) * GROUP, GROUP), :] = values[x]

    return emit


def early_kernel(planes, nx, own_ref, level_ref, core_ref, first_ref, field, levels, y_ref):
    plane_rows = nx * GROUP
    field[pl.ds(0, planes * plane_rows), :] = own_ref[...]
    place_planes(core_ref, planes, field, 2 * planes - 1, -1, plane_rows)
    add_low(core_ref, planes, field, planes, plane_rows)
    levels[pl.ds(0, planes * nx), :] = level_ref[...]
    place_levels(core_ref, planes, nx, levels, 2 * planes - 1, -1, planes - NEAR)
    matrix = circulant(y_ref.shape[1])
    apply_planes(
        matrix, field, WIDTH, 2 * planes - 2 * WIDTH, nx, y_ref, levels, WIDTH, True,
        store_planes(first_ref, 0, nx),
    )


def middle_kernel(
    planes, nx, own_ref, level_ref, chip_ref, early_ref, first_ref, second_ref, core_ref,
    field, levels, first, y_ref,
):
    plane_rows = nx * GROUP
    size = planes * plane_rows
    side = WIDTH * plane_rows
    place_planes(chip_ref, planes, field, planes - 1, -1, plane_rows)
    add_low(chip_ref, planes, field, planes - 1, plane_rows)
    field[pl.ds(size, size), :] = own_ref[...]
    place_levels(chip_ref, planes, nx, levels, planes - 1, -1, 0)
    levels[pl.ds(planes * nx, planes * nx), :] = level_ref[...]
    matrix = circulant(y_ref.shape[1])

    def emit_first(i, values, center):
        for x in range(nx):
            at = aligned((i * nx + x) * GROUP, GROUP)
            first_ref[at, :] = values[x]
            first[at, :] = values[x]

    begin = planes - WIDTH
    apply_planes(matrix, field, begin, planes, nx, y_ref, levels, begin, True, emit_first)
    first[pl.ds(planes * plane_rows, planes * plane_rows), :] = early_ref[...]

    def emit_second(i, values, center):
        for x in range(nx):
            at = aligned((i * nx + x) * GROUP, GROUP)
            second_ref[at, :] = 2.0 * values[x] - own_ref[at, :]

    apply_planes(matrix, first, WIDTH, planes, nx, y_ref, levels, planes, True, emit_second)
    core_ref[...] = second_ref[pl.ds(size - side, side), :].astype(BF16)


def forward_kernel(begin, early_ref, chip_ref, far_ref):
    del early_ref
    far_ref[...] = chip_ref[pl.ds(begin, far_ref.shape[0]), :]


def left_kernel(
    planes, nx, level_ref, chip_ref, far_ref, middle_ref, second_ref,
    pairs_ref, filtered_hbm, field, levels, first, second, y_ref, filtered, semaphore,
):
    plane_rows = nx * GROUP
    rows = planes * nx
    size = planes * plane_rows
    side = WIDTH * plane_rows
    odd = lax.rem(lax.axis_index("space"), 2)

    @pl.loop(0, planes)
    def _(plane):
        target = lax.select(odd == 1, planes - 1 - plane, plane) * nx
        for x in range(nx):
            value = second_ref[aligned((plane * nx + x) * GROUP, GROUP), :]
            filtered[pl.ds(target + x, GROUP, stride=rows), :] = value

    write = pltpu.make_async_copy(filtered, filtered_hbm, semaphore)
    write.start()
    matrix = circulant(y_ref.shape[1])

    field[pl.ds(0, side), :] = far_ref[...].astype(F32)
    place_planes(chip_ref, planes, field, WIDTH + planes - 1, -1, plane_rows)
    add_low(chip_ref, planes, field, WIDTH + planes - 1, plane_rows)
    place_levels(chip_ref, planes, nx, levels, planes - 1, -1, 0)
    first[pl.ds(side, size), :] = middle_ref[...]
    second[pl.ds(side, size), :] = second_ref[...]
    apply_planes(
        matrix, field, WIDTH, WIDTH, nx, y_ref, levels, 0, True, store_planes(first, 0, nx)
    )

    def emit_second(i, values, center):
        for x in range(nx):
            row = (i * nx + x) * GROUP
            before = field[aligned(planes * plane_rows + row, GROUP), :]
            second[aligned(row, GROUP), :] = 2.0 * values[x] - before

    apply_planes(
        matrix, first, WIDTH, WIDTH, nx, y_ref, levels, planes - WIDTH, True, emit_second
    )
    apply_planes(
        matrix, second, WIDTH, WIDTH, nx, y_ref, level_ref, 0, False, store_pairs(pairs_ref, nx)
    )
    write.wait()


def store_pairs(ref, nx):
    def emit(i, values, center):
        for x in range(nx):
            pair = jnp.concatenate([center[x], values[x]], axis=0).astype(BF16)
            ref[aligned((i * nx + x) * 2 * GROUP, 2 * GROUP), :] = pair

    return emit


def right_kernel(
    planes, nx, level_ref, core_ref, second_ref, left_ref, out_ref, second, y_ref, pairs,
):
    plane_rows = nx * GROUP
    size = planes * plane_rows
    band, height, _ = out_ref.shape
    me = lax.axis_index("band")
    second[pl.ds(0, size), :] = second_ref[...]
    place_planes(core_ref, WIDTH, second, planes + WIDTH - 1, -1, plane_rows)
    matrix = circulant(y_ref.shape[1])
    half = planes - WIDTH
    apply_planes(
        matrix, second, WIDTH, half, nx, y_ref, level_ref, WIDTH, False, store_pairs(pairs, nx)
    )
    for i in range(band // 2):
        at = pl.ds(i * height, height)
        out_ref[i ^ me] = left_ref[at, :]
        out_ref[(band // 2 + i) ^ me] = pairs[at, :]


def gram_kernel(space, steps, *refs):
    *blocks, out_ref, held = refs
    band = len(blocks)
    width = 2 * GROUP
    me = lax.axis_index("band")
    for k in range(band):
        held[k ^ me] = blocks[k][...]
    total = jnp.zeros((band * width, band * width), F32)
    for step in range(0, steps, 2):
        block = jnp.concatenate(
            [held[:, pl.ds((step + i) * width, width), :].reshape(band * width, -1) for i in range(2)],
            axis=1,
        )
        total = total + lax.dot_general(
            block, block, (((1,), (1,)), ((), ())), preferred_element_type=F32
        )
    lanes = lax.broadcasted_iota(jnp.int32, (GROUP, band * width), 1)
    for b in range(band):
        narrow = total[b * width : b * width + GROUP]
        applied = pltpu.roll(total[b * width + GROUP : (b + 1) * width], GROUP, 1)
        piece = jnp.where(lanes % width < GROUP, narrow, applied)
        for s in range(space):
            out_ref[s * band + b] = piece


def sum_kernel(scale, in_ref, intersection_ref, projected_ref):
    total = in_ref[0]
    for i in range(1, in_ref.shape[0]):
        total = total + in_ref[i]
    total = total * scale
    lanes, columns = total.shape[1], intersection_ref.shape[1]
    source = lax.broadcasted_iota(jnp.int32, (lanes, columns), 0)
    target = lax.broadcasted_iota(jnp.int32, (lanes, columns), 1)
    place = (target // GROUP) * (2 * GROUP) + target % GROUP
    for offset, ref in ((0, intersection_ref), (GROUP, projected_ref)):
        pick = jnp.where(source == place + offset, 1.0, 0.0).astype(F32)
        ref[...] = jnp.dot(total, pick, precision=lax.Precision.HIGHEST, preferred_element_type=F32)


def call(kernel, outs, *args, scratch=(), hbm_in=0, hbm_out=(), space=pl.ANY, flops=1000000):
    anywhere = pl.BlockSpec(memory_space=space)
    return pl.pallas_call(
        kernel,
        out_shape=outs,
        in_specs=[anywhere] * hbm_in + [VMEM] * (len(args) - hbm_in),
        out_specs=tuple(anywhere if i in hbm_out else VMEM for i in range(len(outs))),
        scratch_shapes=list(scratch),
        compiler_params=PARAMS,
        cost_estimate=pl.CostEstimate(flops=flops, bytes_accessed=1000000, transcendentals=0),
    )(*args)


def shifts(axis):
    count = lax.axis_size(axis)
    up = [(i, (i + 1) % count) for i in range(count)]
    return up, [(j, i) for i, j in up]


def local_kernels(orbitals, potential):
    count, planes, nx, ny = orbitals.shape
    space, band = lax.axis_size("space"), lax.axis_size("band")
    rows = planes * nx
    plane_rows = nx * GROUP
    size = planes * plane_rows
    struct = jax.ShapeDtypeStruct
    other_core = [(i, i ^ 1) for i in range(space)]
    other_chip = [(i, i ^ 3) for i in range(space)]

    def f32_planes(many, height=plane_rows):
        return pltpu.VMEM((many * height, ny), F32)

    message = struct((size + plane_rows + (planes + NEAR) * nx, ny), BF16)
    slab = struct((size, ny), F32)
    parts = 4
    own, levels, to_chip, to_core = call(
        functools.partial(prepare_kernel, planes, nx),
        (slab, struct((rows, ny), F32), message, message),
        orbitals, potential.reshape(rows, ny),
        hbm_in=2, space=pltpu.HBM,
        scratch=[
            pltpu.VMEM(orbitals.shape, F32),
            pltpu.VMEM((rows, ny), F32),
            pltpu.SemaphoreType.DMA((parts + 1,)),
        ],
    )
    chip = lax.ppermute(to_chip, "space", other_chip)
    core = lax.ppermute(to_core, "space", other_core)
    (early,) = call(
        functools.partial(early_kernel, planes, nx),
        (slab,),
        own, levels, core,
        scratch=[f32_planes(2 * planes), f32_planes(2 * planes, nx), f32_planes(planes)],
    )
    side = struct((WIDTH * plane_rows, ny), BF16)
    (far,) = call(
        functools.partial(forward_kernel, (planes - WIDTH) * plane_rows), (side,), early, chip, hbm_in=1
    )
    far = lax.ppermute(far, "space", other_core)
    middle, second, to_core = call(
        functools.partial(middle_kernel, planes, nx),
        (slab, slab, side),
        own, levels, chip, early,
        scratch=[
            f32_planes(2 * planes), f32_planes(2 * planes, nx), f32_planes(2 * planes), f32_planes(planes),
        ],
    )
    beside = lax.ppermute(to_core, "space", other_core)
    left, filtered = call(
        functools.partial(left_kernel, planes, nx),
        (struct((WIDTH * nx * 2 * GROUP, ny), BF16), struct((count * rows, ny), F32)),
        levels, chip, far, middle, second,
        hbm_out=(1,),
        scratch=[
            f32_planes(planes + WIDTH),
            f32_planes(planes, nx),
            f32_planes(planes + WIDTH),
            f32_planes(planes + WIDTH),
            f32_planes(WIDTH),
            pltpu.VMEM((count * rows, ny), F32),
            pltpu.SemaphoreType.DMA,
        ],
    )
    steps = rows // band
    block = (steps * 2 * GROUP, ny)
    (pairs,) = call(
        functools.partial(right_kernel, planes, nx),
        (struct((band, *block), BF16),),
        levels, beside, second, left,
        scratch=[
            f32_planes(planes + WIDTH),
            f32_planes(planes - WIDTH),
            pltpu.VMEM(((planes - WIDTH) * nx * 2 * GROUP, ny), BF16),
        ],
    )
    blocks = [pairs[0]]
    for k in range(1, band):
        blocks.append(lax.ppermute(pairs[k], "band", [(i, i ^ k) for i in range(band)]))
    (pieces,) = call(
        functools.partial(gram_kernel, space, steps),
        (struct((space * band, GROUP, band * 2 * GROUP), F32),),
        *blocks,
        scratch=[pltpu.VMEM((band, *block), BF16)],
    )
    pieces = lax.all_to_all(pieces, ("space", "band"), 0, 0, tiled=True)
    rows_out = struct((count, count * band), F32)
    intersection, projected = call(
        functools.partial(sum_kernel, 1.0 / (rows * ny * space)), (rows_out, rows_out), pieces
    )
    return filtered.reshape(orbitals.shape), intersection, projected


def padded(cells, width):
    up, down = shifts("space")
    head, tail = cells[:, :width], cells[:, cells.shape[1] - width :]
    return jnp.concatenate(
        [lax.ppermute(tail, "space", up), cells, lax.ppermute(head, "space", down)], axis=1
    )


def hamiltonian(beside, potential):
    planes = beside.shape[1] - 2 * WIDTH
    center = beside[:, WIDTH : WIDTH + planes]
    summed = 3.0 * STENCIL[0] * center
    for k in range(1, WIDTH + 1):
        near = beside[:, WIDTH + k : WIDTH + k + planes] + beside[:, WIDTH - k : WIDTH - k + planes]
        for dim in (2, 3):
            near = near + (jnp.roll(center, k, dim) + jnp.roll(center, -k, dim))
        summed = summed + STENCIL[k] * near
    return -0.5 * summed + potential * center


def local_plain(orbitals, potential):
    def step(field):
        return (hamiltonian(padded(field, WIDTH), potential) - 9.0 * field) * 0.125

    filtered = 2.0 * step(step(orbitals)) - orbitals
    beside = padded(filtered.astype(BF16), WIDTH).astype(F32)
    applied = hamiltonian(beside, potential).astype(BF16)
    count = orbitals.shape[0]
    narrow = filtered.astype(BF16).reshape(count, -1)
    applied = applied.reshape(count, -1)
    everyone = lax.all_gather(narrow, "band", axis=0, tiled=True)
    contract = (((1,), (1,)), ((), ()))
    parts = [
        lax.dot_general(rows, everyone, contract, preferred_element_type=F32)
        for rows in (narrow, applied)
    ]
    scale = 1.0 / (narrow.shape[1] * lax.axis_size("space"))
    intersection, projected = lax.psum(tuple(parts), "space")
    return filtered, intersection * scale, projected * scale


def local(orbitals, potential):
    count, planes, nx, ny = orbitals.shape
    band = lax.axis_size("band")
    fits = (
        count == GROUP
        and lax.axis_size("space") == 4
        and planes == 2 * WIDTH
        and nx == 16
        and ny == 128
        and band * 2 * GROUP == 128
        and (planes * nx) % (2 * band) == 0
    )
    return (local_kernels if fits else local_plain)(orbitals, potential)


def solution(mesh):
    return jax.shard_map(
        local,
        mesh=mesh,
        in_specs=(P("band", "space", None, None), P("space", None, None)),
        out_specs=(P("band", "space", None, None), P("band", None), P("band", None)),
        check_vma=False,
    )
```

```python
import functools

import jax
import jax.numpy as jnp
from jax import lax
from jax.experimental import pallas as pl
from jax.experimental.pallas import tpu as pltpu
from jax.sharding import PartitionSpec as P

STENCIL = (
    -5369.0 / 1800.0,
    12.0 / 7.0,
    -15.0 / 56.0,
    10.0 / 189.0,
    -1.0 / 112.0,
    2.0 / 1925.0,
    -1.0 / 16632.0,
)
WIDTH = 6
BF16 = jnp.bfloat16
F32 = jnp.float32
VMEM = pl.BlockSpec(memory_space=pltpu.VMEM)

GROUP = 8

H_FACTORS = tuple(-0.5 * c for c in STENCIL[1:])
H_CENTER = -1.5 * STENCIL[0]
L_FACTORS = tuple(0.125 * c for c in H_FACTORS)
L_CENTER = (H_CENTER - 9.0) / 8.0


def aligned(start, size):
    return pl.ds(pl.multiple_of(start, size), size)


def low_part(block):
    return block - block.astype(BF16).astype(F32)


def circulant(ny):
    row = lax.broadcasted_iota(jnp.int32, (ny, ny), 0)
    column = lax.broadcasted_iota(jnp.int32, (ny, ny), 1)
    apart = jnp.abs(row - column)
    apart = jnp.minimum(apart, ny - apart)
    matrix = jnp.zeros((ny, ny), F32)
    for k in range(1, WIDTH + 1):
        matrix = jnp.where(apart == k, H_FACTORS[k - 1] / H_FACTORS[0], matrix)
    matrix = matrix.astype(BF16)
    return jnp.concatenate([matrix, matrix], axis=0)


def along_y(matrix, source, start, count, y_ref, plane_rows):
    step = min(count, WIDTH)
    for i in range(0, count, step):
        block = source[pl.ds((start + i) * plane_rows, step * plane_rows), :]
        parts = jnp.concatenate([block.astype(BF16), low_part(block).astype(BF16)], axis=1)
        y_ref[pl.ds(i * plane_rows, step * plane_rows), :] = jnp.dot(
            parts, matrix, preferred_element_type=F32
        )


def apply_planes(matrix, source, start, count, nx, y_ref, levels, level, linear, emit):
    plane_rows = nx * GROUP
    along_y(matrix, source, start, count, y_ref, plane_rows)
    factors = L_FACTORS if linear else H_FACTORS

    def load(row):
        return source[aligned(row, GROUP), :]

    @pl.loop(0, count)
    def _(i):
        where = (start + i) * plane_rows
        center = [load(where + x * GROUP) for x in range(nx)]
        values = []
        for x in range(nx):
            row = levels[pl.ds((level + i) * nx + x, 1), :]
            row = 0.125 * row + L_CENTER if linear else row + H_CENTER
            total = jnp.broadcast_to(row, center[x].shape) * center[x]
            total = total + factors[0] * y_ref[aligned(i * plane_rows + x * GROUP, GROUP), :]
            for k in range(1, WIDTH + 1):
                near = load(where + k * plane_rows + x * GROUP) + load(where - k * plane_rows + x * GROUP)
                near = near + (center[(x + k) % nx] + center[(x - k) % nx])
                total = total + factors[k - 1] * near
            values.append(total)
        emit(i, values, center)


def prepare_kernel(
    planes, nx, orbitals_hbm, potential_hbm, own_ref, level_ref, near_ref, far_ref, core_ref,
    orbitals, potential, semaphores,
):
    plane_rows = nx * GROUP
    rows = planes * nx
    side = WIDTH * plane_rows
    parts = semaphores.shape[0] - 1
    each = planes // parts
    odd = lax.rem(lax.axis_index("space"), 2)

    def fetch(i):
        at = pl.ds(i * each, each)
        return pltpu.make_async_copy(orbitals_hbm.at[:, at], orbitals.at[:, at], semaphores.at[i])

    fetch_levels = pltpu.make_async_copy(potential_hbm, potential, semaphores.at[parts])
    for i in range(parts):
        fetch(i).start()
    fetch_levels.start()
    cells = orbitals.reshape(GROUP * rows, orbitals.shape[-1])
    for i in range(parts):
        fetch(i).wait()

        @pl.loop(i * each, (i + 1) * each)
        def _(plane):
            target = lax.select(odd == 1, planes - 1 - plane, plane) * plane_rows
            for x in range(0, nx, 2):
                row = plane * nx + x
                both = jnp.concatenate(
                    [cells[pl.ds(row + j, GROUP, stride=rows), :] for j in range(2)], axis=0
                )
                at = aligned(target + x * GROUP, 2 * GROUP)
                own_ref[at, :] = both
                core_ref[at, :] = both.astype(BF16)

    near_ref[pl.ds(0, side), :] = core_ref[pl.ds(0, side), :]
    far_ref[pl.ds(0, side), :] = core_ref[pl.ds(side, side), :]
    size = planes * plane_rows
    for out_ref, plane, at in ((near_ref, 0, side), (core_ref, planes - 1, size)):
        block = own_ref[pl.ds(plane * plane_rows, plane_rows), :]
        out_ref[pl.ds(at, plane_rows), :] = low_part(block).astype(BF16)
    fetch_levels.wait()
    for plane in range(planes):
        source = lax.select(odd == 1, planes - 1 - plane, plane) * nx
        block = potential[aligned(source, nx), :]
        level_ref[pl.ds(plane * nx, nx), :] = block
        core_ref[pl.ds(size + plane_rows + plane * nx, nx), :] = block.astype(BF16)
        if plane < WIDTH:
            near_ref[pl.ds(side + plane_rows + plane * nx, nx), :] = block.astype(BF16)
        else:
            far_ref[pl.ds(side + (plane - WIDTH) * nx, nx), :] = block.astype(BF16)
        if plane < NEAR:
            at = side + plane_rows + (WIDTH + plane) * nx
            near_ref[pl.ds(at, nx), :] = low_part(block).astype(BF16)
        if plane >= planes - NEAR:
            at = size + plane_rows + (planes + plane - (planes - NEAR)) * nx
            core_ref[pl.ds(at, nx), :] = low_part(block).astype(BF16)


NEAR = 2


def place_planes(message, count, field, where, step, plane_rows):
    for i in range(count):
        block = message[pl.ds(i * plane_rows, plane_rows), :]
        field[pl.ds((where + step * i) * plane_rows, plane_rows), :] = block.astype(F32)


def add_low(message, planes, field, where, plane_rows):
    at = pl.ds(where * plane_rows, plane_rows)
    field[at, :] = field[at, :] + message[pl.ds(planes * plane_rows, plane_rows), :].astype(F32)


def place_levels(message, extra, count, nx, levels, where, near):
    for i in range(count):
        block = message[pl.ds(extra + i * nx, nx), :].astype(F32)
        if near <= i < near + NEAR:
            block = block + message[pl.ds(extra + (count + i - near) * nx, nx), :].astype(F32)
        levels[pl.ds((where - i) * nx, nx), :] = block


def store_planes(nx, *refs):
    def emit(i, values, center):
        for x in range(nx):
            for ref, first in refs:
                ref[aligned(((first + i) * nx + x) * GROUP, GROUP), :] = values[x]

    return emit


def store_second(nx, before, start, *refs):
    def emit(i, values, center):
        for x in range(nx):
            row = (i * nx + x) * GROUP
            value = 2.0 * values[x] - before[aligned(start * nx * GROUP + row, GROUP), :]
            for ref, first in refs:
                ref[aligned(first * nx * GROUP + row, GROUP), :] = value

    return emit


def early_kernel(planes, nx, own_ref, level_ref, core_ref, first_ref, field, levels, y_ref):
    plane_rows = nx * GROUP
    field[pl.ds(0, planes * plane_rows), :] = own_ref[...]
    place_planes(core_ref, planes, field, 2 * planes - 1, -1, plane_rows)
    add_low(core_ref, planes, field, planes, plane_rows)
    levels[pl.ds(0, planes * nx), :] = level_ref[...]
    extra = (planes + 1) * plane_rows
    place_levels(core_ref, extra, planes, nx, levels, 2 * planes - 1, planes - NEAR)
    matrix = circulant(y_ref.shape[1])
    apply_planes(
        matrix, field, WIDTH, 2 * planes - 2 * WIDTH, nx, y_ref, levels, WIDTH, True,
        store_planes(nx, (first_ref, 0)),
    )


def pass_kernel(after_ref, in_ref, out_ref):
    del after_ref
    out_ref[...] = in_ref[...]


def near_kernel(
    planes, nx, own_ref, level_ref, near_ref, early_ref, first_ref, second_ref, core_ref,
    field, first, y_ref,
):
    plane_rows = nx * GROUP
    side = WIDTH * plane_rows
    place_planes(near_ref, WIDTH, field, WIDTH - 1, -1, plane_rows)
    add_low(near_ref, WIDTH, field, WIDTH - 1, plane_rows)
    field[pl.ds(side, 2 * side), :] = own_ref[...]
    first[pl.ds(side, 2 * side), :] = early_ref[...]
    matrix = circulant(y_ref.shape[1])
    apply_planes(
        matrix, field, WIDTH, WIDTH, nx, y_ref, level_ref, 0, True,
        store_planes(nx, (first_ref, 0), (first, 0)),
    )
    apply_planes(
        matrix, first, WIDTH, WIDTH, nx, y_ref, level_ref, WIDTH, True,
        store_second(nx, own_ref, WIDTH, (second_ref, 0)),
    )
    core_ref[...] = second_ref[...].astype(BF16)


def middle_kernel(
    planes, nx, own_ref, level_ref, near_ref, far_ref, early_ref, beside_first_ref,
    first_ref, second_ref, field, levels, first, y_ref,
):
    plane_rows = nx * GROUP
    side = WIDTH * plane_rows
    place_planes(far_ref, WIDTH, field, WIDTH - 1, -1, plane_rows)
    place_planes(near_ref, WIDTH, field, planes - 1, -1, plane_rows)
    add_low(near_ref, WIDTH, field, planes - 1, plane_rows)
    field[pl.ds(2 * side, side), :] = own_ref[pl.ds(0, side), :]
    place_levels(near_ref, side + plane_rows, WIDTH, nx, levels, WIDTH - 1, 0)
    first[pl.ds(side, side), :] = beside_first_ref[...]
    first[pl.ds(2 * side, side), :] = early_ref[pl.ds(0, side), :]
    matrix = circulant(y_ref.shape[1])
    apply_planes(
        matrix, field, WIDTH, WIDTH, nx, y_ref, levels, 0, True,
        store_planes(nx, (first_ref, 0), (first, 0)),
    )
    apply_planes(
        matrix, first, WIDTH, WIDTH, nx, y_ref, level_ref, 0, True,
        store_second(nx, own_ref, 0, (second_ref, 0)),
    )


def right_kernel(
    planes, nx, level_ref, beside_ref, second_ref, beyond_ref, pairs_ref, second, y_ref,
):
    plane_rows = nx * GROUP
    side = WIDTH * plane_rows
    second[pl.ds(0, side), :] = second_ref[...]
    second[pl.ds(side, side), :] = beyond_ref[...]
    place_planes(beside_ref, WIDTH, second, 3 * WIDTH - 1, -1, plane_rows)
    matrix = circulant(y_ref.shape[1])
    apply_planes(
        matrix, second, WIDTH, WIDTH, nx, y_ref, level_ref, WIDTH, False, store_pairs(pairs_ref, 0, nx)
    )


def left_kernel(
    planes, nx, level_ref, near_ref, far_ref, relay_ref, first_low_ref, first_ref, second_ref,
    beyond_ref, right_ref, out_ref, field, levels, first, second, y_ref, pairs,
):
    plane_rows = nx * GROUP
    side = WIDTH * plane_rows
    place_planes(relay_ref, WIDTH, field, 0, 1, plane_rows)
    place_planes(far_ref, WIDTH, field, 2 * WIDTH - 1, -1, plane_rows)
    place_planes(near_ref, WIDTH, field, 3 * WIDTH - 1, -1, plane_rows)
    add_low(near_ref, WIDTH, field, 3 * WIDTH - 1, plane_rows)
    place_levels(far_ref, side, WIDTH, nx, levels, WIDTH - 1, WIDTH)
    place_levels(near_ref, side + plane_rows, WIDTH, nx, levels, 2 * WIDTH - 1, 0)
    first[pl.ds(side, side), :] = first_low_ref[...]
    first[pl.ds(2 * side, side), :] = first_ref[...]
    second[pl.ds(side, side), :] = second_ref[...]
    second[pl.ds(2 * side, side), :] = beyond_ref[...]
    matrix = circulant(y_ref.shape[1])
    apply_planes(
        matrix, field, WIDTH, WIDTH, nx, y_ref, levels, 0, True, store_planes(nx, (first, 0))
    )
    apply_planes(
        matrix, first, WIDTH, WIDTH, nx, y_ref, levels, WIDTH, True,
        store_second(nx, field, 2 * WIDTH, (second, 0)),
    )
    apply_planes(
        matrix, second, WIDTH, WIDTH, nx, y_ref, level_ref, 0, False, store_pairs(pairs, 0, nx)
    )
    band, height, _ = out_ref.shape
    me = lax.axis_index("band")
    for i in range(band // 2):
        at = pl.ds(i * height, height)
        out_ref[i ^ me] = pairs[at, :]
        out_ref[(band // 2 + i) ^ me] = right_ref[at, :]


def write_kernel(planes, nx, second_ref, beyond_ref, filtered_ref, done_ref):
    done_ref[...] = jnp.zeros_like(done_ref)
    rows = planes * nx
    odd = lax.rem(lax.axis_index("space"), 2)
    for ref, first in ((second_ref, 0), (beyond_ref, WIDTH)):

        @pl.loop(0, WIDTH)
        def _(i):
            plane = first + i
            target = lax.select(odd == 1, planes - 1 - plane, plane) * nx
            for x in range(nx):
                value = ref[aligned((i * nx + x) * GROUP, GROUP), :]
                filtered_ref[pl.ds(target + x, GROUP, stride=rows), :] = value


def store_pairs(ref, first, nx):
    def emit(i, values, center):
        for x in range(nx):
            pair = jnp.concatenate([center[x], values[x]], axis=0).astype(BF16)
            ref[aligned(((first + i) * nx + x) * 2 * GROUP, 2 * GROUP), :] = pair

    return emit


def gram_kernel(space, steps, order, *refs):
    after_ref, *blocks, out_ref, held = refs
    del after_ref
    band = len(blocks)
    width = 2 * GROUP
    me = lax.axis_index("band")
    for k, block in zip(order, blocks):
        held[k ^ me] = block[...]
    total = jnp.zeros((band * width, band * width), F32)
    for step in range(0, steps, 2):
        block = jnp.concatenate(
            [held[:, pl.ds((step + i) * width, width), :].reshape(band * width, -1) for i in range(2)],
            axis=1,
        )
        total = total + lax.dot_general(
            block, block, (((1,), (1,)), ((), ())), preferred_element_type=F32
        )
    lanes = lax.broadcasted_iota(jnp.int32, (GROUP, band * width), 1)
    for b in range(band):
        narrow = total[b * width : b * width + GROUP]
        applied = pltpu.roll(total[b * width + GROUP : (b + 1) * width], GROUP, 1)
        piece = jnp.where(lanes % width < GROUP, narrow, applied)
        for s in range(space):
            out_ref[s * band + b] = piece


def sum_kernel(scale, in_ref, intersection_ref, projected_ref):
    total = in_ref[0]
    for i in range(1, in_ref.shape[0]):
        total = total + in_ref[i]
    total = total * scale
    lanes, columns = total.shape[1], intersection_ref.shape[1]
    source = lax.broadcasted_iota(jnp.int32, (lanes, columns), 0)
    target = lax.broadcasted_iota(jnp.int32, (lanes, columns), 1)
    place = (target // GROUP) * (2 * GROUP) + target % GROUP
    for offset, ref in ((0, intersection_ref), (GROUP, projected_ref)):
        pick = jnp.where(source == place + offset, 1.0, 0.0).astype(F32)
        ref[...] = jnp.dot(total, pick, precision=lax.Precision.HIGHEST, preferred_element_type=F32)


ORDER = (1, 2, 4, 6, 5, 7, 3)


def call(kernel, outs, *args, scratch=(), hbm_in=0, hbm_out=(), vmem=40, flops=1000000):
    anywhere = pl.BlockSpec(memory_space=pl.ANY)
    return pl.pallas_call(
        kernel,
        out_shape=outs,
        in_specs=[anywhere] * hbm_in + [VMEM] * (len(args) - hbm_in),
        out_specs=tuple(anywhere if i in hbm_out else VMEM for i in range(len(outs))),
        scratch_shapes=list(scratch),
        compiler_params=pltpu.CompilerParams(vmem_limit_bytes=int(vmem * 2**20)),
        cost_estimate=pl.CostEstimate(flops=flops, bytes_accessed=1000000, transcendentals=0),
    )(*args)


def shifts(axis):
    count = lax.axis_size(axis)
    up = [(i, (i + 1) % count) for i in range(count)]
    return up, [(j, i) for i, j in up]


def local_kernels(orbitals, potential):
    count, planes, nx, ny = orbitals.shape
    space, band = lax.axis_size("space"), lax.axis_size("band")
    rows = planes * nx
    plane_rows = nx * GROUP
    size = planes * plane_rows
    struct = jax.ShapeDtypeStruct
    other_core = [(i, i ^ 1) for i in range(space)]
    other_chip = [(i, i ^ 3) for i in range(space)]

    def f32_planes(many, height=plane_rows):
        return pltpu.VMEM((many * height, ny), F32)

    def bf16_rows(height):
        return struct((height, ny), BF16)

    half = WIDTH * plane_rows
    slab, half_slab = struct((size, ny), F32), struct((half, ny), F32)
    parts = 4
    own, levels, to_near, to_far, to_core = call(
        functools.partial(prepare_kernel, planes, nx),
        (
            slab,
            struct((rows, ny), F32),
            bf16_rows(half + plane_rows + (WIDTH + NEAR) * nx),
            bf16_rows(half + WIDTH * nx),
            bf16_rows(size + plane_rows + (planes + NEAR) * nx),
        ),
        orbitals, potential.reshape(rows, ny),
        hbm_in=2, vmem=52,
        scratch=[
            pltpu.VMEM(orbitals.shape, F32),
            pltpu.VMEM((rows, ny), F32),
            pltpu.SemaphoreType.DMA((parts + 1,)),
        ],
    )
    near = lax.ppermute(to_near, "space", other_chip)
    core = lax.ppermute(to_core, "space", other_core)
    far = lax.ppermute(to_far, "space", other_chip)
    (early,) = call(
        functools.partial(early_kernel, planes, nx),
        (slab,),
        own, levels, core,
        scratch=[f32_planes(2 * planes), f32_planes(2 * planes, nx), f32_planes(planes)],
    )
    wide = planes + WIDTH
    first, beyond, to_beside = call(
        functools.partial(near_kernel, planes, nx),
        (half_slab, half_slab, bf16_rows(half)),
        own, levels, near, early,
        scratch=[f32_planes(wide), f32_planes(wide), f32_planes(WIDTH)],
    )
    beside = lax.ppermute(to_beside, "space", other_core)
    (relay,) = call(pass_kernel, (bf16_rows(half + WIDTH * nx),), first, far, hbm_in=1)
    relay = lax.ppermute(relay, "space", other_core)
    first_low, second = call(
        functools.partial(middle_kernel, planes, nx),
        (half_slab, half_slab),
        own, levels, near, far, early, first,
        scratch=[f32_planes(wide), f32_planes(WIDTH, nx), f32_planes(wide), f32_planes(WIDTH)],
    )
    (right,) = call(
        functools.partial(right_kernel, planes, nx),
        (bf16_rows(WIDTH * nx * 2 * GROUP),),
        levels, beside, second, beyond,
        scratch=[f32_planes(wide), f32_planes(WIDTH)],
    )
    steps = rows // band
    block = (steps * 2 * GROUP, ny)
    (pairs,) = call(
        functools.partial(left_kernel, planes, nx),
        (struct((band, *block), BF16),),
        levels, near, far, relay, first_low, first, second, beyond, right,
        scratch=[
            f32_planes(wide),
            f32_planes(planes, nx),
            f32_planes(wide),
            f32_planes(wide),
            f32_planes(WIDTH),
            pltpu.VMEM((WIDTH * nx * 2 * GROUP, ny), BF16),
        ],
    )
    filtered, written = call(
        functools.partial(write_kernel, planes, nx),
        (struct((count * rows, ny), F32), struct((GROUP, ny), F32)),
        second, beyond,
    )
    order = (0,) + ORDER[::-1]
    blocks = [
        lax.ppermute(pairs[k], "band", [(i, i ^ k) for i in range(band)]) if k else pairs[k]
        for k in order
    ]
    (pieces,) = call(
        functools.partial(gram_kernel, space, steps, order),
        (struct((space * band, GROUP, band * 2 * GROUP), F32),),
        written, *blocks,
        hbm_in=1,
        scratch=[pltpu.VMEM((band, *block), BF16)],
    )
    pieces = lax.all_to_all(pieces, ("space", "band"), 0, 0, tiled=True)
    rows_out = struct((count, count * band), F32)
    intersection, projected = call(
        functools.partial(sum_kernel, 1.0 / (rows * ny * space)), (rows_out, rows_out), pieces
    )
    return filtered.reshape(orbitals.shape), intersection, projected


def padded(cells, width):
    up, down = shifts("space")
    head, tail = cells[:, :width], cells[:, cells.shape[1] - width :]
    return jnp.concatenate(
        [lax.ppermute(tail, "space", up), cells, lax.ppermute(head, "space", down)], axis=1
    )


def hamiltonian(beside, potential):
    planes = beside.shape[1] - 2 * WIDTH
    center = beside[:, WIDTH : WIDTH + planes]
    summed = 3.0 * STENCIL[0] * center
    for k in range(1, WIDTH + 1):
        near = beside[:, WIDTH + k : WIDTH + k + planes] + beside[:, WIDTH - k : WIDTH - k + planes]
        for dim in (2, 3):
            near = near + (jnp.roll(center, k, dim) + jnp.roll(center, -k, dim))
        summed = summed + STENCIL[k] * near
    return -0.5 * summed + potential * center


def local_plain(orbitals, potential):
    def step(field):
        return (hamiltonian(padded(field, WIDTH), potential) - 9.0 * field) * 0.125

    filtered = 2.0 * step(step(orbitals)) - orbitals
    beside = padded(filtered.astype(BF16), WIDTH).astype(F32)
    applied = hamiltonian(beside, potential).astype(BF16)
    count = orbitals.shape[0]
    narrow = filtered.astype(BF16).reshape(count, -1)
    applied = applied.reshape(count, -1)
    everyone = lax.all_gather(narrow, "band", axis=0, tiled=True)
    contract = (((1,), (1,)), ((), ()))
    parts = [
        lax.dot_general(rows, everyone, contract, preferred_element_type=F32)
        for rows in (narrow, applied)
    ]
    scale = 1.0 / (narrow.shape[1] * lax.axis_size("space"))
    intersection, projected = lax.psum(tuple(parts), "space")
    return filtered, intersection * scale, projected * scale


def local(orbitals, potential):
    count, planes, nx, ny = orbitals.shape
    band = lax.axis_size("band")
    fits = (
        count == GROUP
        and lax.axis_size("space") == 4
        and planes == 2 * WIDTH
        and nx == 16
        and ny == 128
        and band * 2 * GROUP == 128
        and (planes * nx) % (2 * band) == 0
    )
    return (local_kernels if fits else local_plain)(orbitals, potential)


def solution(mesh):
    return jax.shard_map(
        local,
        mesh=mesh,
        in_specs=(P("band", "space", None, None), P("space", None, None)),
        out_specs=(P("band", "space", None, None), P("band", None), P("band", None)),
        check_vma=False,
    )
```

```python
import functools

import jax
import jax.numpy as jnp
from jax import lax
from jax.experimental import pallas as pl
from jax.experimental.pallas import tpu as pltpu
from jax.sharding import PartitionSpec as P

STENCIL = (
    -5369.0 / 1800.0,
    12.0 / 7.0,
    -15.0 / 56.0,
    10.0 / 189.0,
    -1.0 / 112.0,
    2.0 / 1925.0,
    -1.0 / 16632.0,
)
WIDTH = 6
BF16 = jnp.bfloat16
F32 = jnp.float32
VMEM = pl.BlockSpec(memory_space=pltpu.VMEM)

GROUP = 8

H_FACTORS = tuple(-0.5 * c for c in STENCIL[1:])
H_CENTER = -1.5 * STENCIL[0]
L_FACTORS = tuple(0.125 * c for c in H_FACTORS)
L_CENTER = (H_CENTER - 9.0) / 8.0


def aligned(start, size):
    return pl.ds(pl.multiple_of(start, size), size)


def low_part(block):
    return block - block.astype(BF16).astype(F32)


def circulant(ny):
    row = lax.broadcasted_iota(jnp.int32, (ny, ny), 0)
    column = lax.broadcasted_iota(jnp.int32, (ny, ny), 1)
    apart = jnp.abs(row - column)
    apart = jnp.minimum(apart, ny - apart)
    matrix = jnp.zeros((ny, ny), F32)
    for k in range(1, WIDTH + 1):
        matrix = jnp.where(apart == k, H_FACTORS[k - 1] / H_FACTORS[0], matrix)
    matrix = matrix.astype(BF16)
    return jnp.concatenate([matrix, matrix], axis=0)


def along_y(matrix, source, start, count, y_ref, plane_rows):
    step = min(count, WIDTH)
    for i in range(0, count, step):
        block = source[pl.ds((start + i) * plane_rows, step * plane_rows), :]
        parts = jnp.concatenate([block.astype(BF16), low_part(block).astype(BF16)], axis=1)
        y_ref[pl.ds(i * plane_rows, step * plane_rows), :] = jnp.dot(
            parts, matrix, preferred_element_type=F32
        )


def apply_planes(matrix, source, start, count, nx, y_ref, levels, level, linear, emit):
    plane_rows = nx * GROUP
    along_y(matrix, source, start, count, y_ref, plane_rows)
    factors = L_FACTORS if linear else H_FACTORS

    def load(row):
        return source[aligned(row, GROUP), :]

    @pl.loop(0, count)
    def _(i):
        where = (start + i) * plane_rows
        center = [load(where + x * GROUP) for x in range(nx)]
        values = []
        for x in range(nx):
            row = levels[pl.ds((level + i) * nx + x, 1), :]
            row = 0.125 * row + L_CENTER if linear else row + H_CENTER
            total = jnp.broadcast_to(row, center[x].shape) * center[x]
            total = total + factors[0] * y_ref[aligned(i * plane_rows + x * GROUP, GROUP), :]
            for k in range(1, WIDTH + 1):
                near = load(where + k * plane_rows + x * GROUP) + load(where - k * plane_rows + x * GROUP)
                near = near + (center[(x + k) % nx] + center[(x - k) % nx])
                total = total + factors[k - 1] * near
            values.append(total)
        emit(i, values, center)


def prepare_kernel(
    planes, nx, orbitals_hbm, potential_hbm, own_ref, level_ref, near_ref, far_ref, core_ref,
    orbitals, potential, semaphores,
):
    plane_rows = nx * GROUP
    rows = planes * nx
    side = WIDTH * plane_rows
    parts = semaphores.shape[0] - 1
    each = planes // parts
    odd = lax.rem(lax.axis_index("space"), 2)

    def fetch(i):
        at = pl.ds(i * each, each)
        return pltpu.make_async_copy(orbitals_hbm.at[:, at], orbitals.at[:, at], semaphores.at[i])

    fetch_levels = pltpu.make_async_copy(potential_hbm, potential, semaphores.at[parts])
    for i in range(parts):
        fetch(i).start()
    fetch_levels.start()
    cells = orbitals.reshape(GROUP * rows, orbitals.shape[-1])
    for i in range(parts):
        fetch(i).wait()

        @pl.loop(i * each, (i + 1) * each)
        def _(plane):
            target = lax.select(odd == 1, planes - 1 - plane, plane) * plane_rows
            for x in range(0, nx, 2):
                row = plane * nx + x
                both = jnp.concatenate(
                    [cells[pl.ds(row + j, GROUP, stride=rows), :] for j in range(2)], axis=0
                )
                at = aligned(target + x * GROUP, 2 * GROUP)
                own_ref[at, :] = both
                core_ref[at, :] = both.astype(BF16)

    near_ref[pl.ds(0, side), :] = core_ref[pl.ds(0, side), :]
    far_ref[pl.ds(0, side), :] = core_ref[pl.ds(side, side), :]
    size = planes * plane_rows
    for out_ref, plane, at in ((near_ref, 0, side), (core_ref, planes - 1, size)):
        block = own_ref[pl.ds(plane * plane_rows, plane_rows), :]
        out_ref[pl.ds(at, plane_rows), :] = low_part(block).astype(BF16)
    fetch_levels.wait()
    for plane in range(planes):
        source = lax.select(odd == 1, planes - 1 - plane, plane) * nx
        block = potential[aligned(source, nx), :]
        level_ref[pl.ds(plane * nx, nx), :] = block
        core_ref[pl.ds(size + plane_rows + plane * nx, nx), :] = block.astype(BF16)
        if plane < WIDTH:
            near_ref[pl.ds(side + plane_rows + plane * nx, nx), :] = block.astype(BF16)
        else:
            far_ref[pl.ds(side + (plane - WIDTH) * nx, nx), :] = block.astype(BF16)
        if plane < NEAR:
            at = side + plane_rows + (WIDTH + plane) * nx
            near_ref[pl.ds(at, nx), :] = low_part(block).astype(BF16)
        if plane >= planes - NEAR:
            at = size + plane_rows + (planes + plane - (planes - NEAR)) * nx
            core_ref[pl.ds(at, nx), :] = low_part(block).astype(BF16)


NEAR = 2


def place_planes(message, count, field, where, step, plane_rows):
    for i in range(count):
        block = message[pl.ds(i * plane_rows, plane_rows), :]
        field[pl.ds((where + step * i) * plane_rows, plane_rows), :] = block.astype(F32)


def add_low(message, planes, field, where, plane_rows):
    at = pl.ds(where * plane_rows, plane_rows)
    field[at, :] = field[at, :] + message[pl.ds(planes * plane_rows, plane_rows), :].astype(F32)


def place_levels(message, extra, count, nx, levels, where, near):
    for i in range(count):
        block = message[pl.ds(extra + i * nx, nx), :].astype(F32)
        if near <= i < near + NEAR:
            block = block + message[pl.ds(extra + (count + i - near) * nx, nx), :].astype(F32)
        levels[pl.ds((where - i) * nx, nx), :] = block


def store_planes(nx, *refs):
    def emit(i, values, center):
        for x in range(nx):
            for ref, first in refs:
                ref[aligned(((first + i) * nx + x) * GROUP, GROUP), :] = values[x]

    return emit


def store_second(nx, before, start, *refs):
    def emit(i, values, center):
        for x in range(nx):
            row = (i * nx + x) * GROUP
            value = 2.0 * values[x] - before[aligned(start * nx * GROUP + row, GROUP), :]
            for ref, first in refs:
                ref[aligned(first * nx * GROUP + row, GROUP), :] = value

    return emit


def early_kernel(planes, nx, own_ref, level_ref, core_ref, first_ref, field, levels, y_ref):
    plane_rows = nx * GROUP
    field[pl.ds(0, planes * plane_rows), :] = own_ref[...]
    place_planes(core_ref, planes, field, 2 * planes - 1, -1, plane_rows)
    add_low(core_ref, planes, field, planes, plane_rows)
    levels[pl.ds(0, planes * nx), :] = level_ref[...]
    extra = (planes + 1) * plane_rows
    place_levels(core_ref, extra, planes, nx, levels, 2 * planes - 1, planes - NEAR)
    matrix = circulant(y_ref.shape[1])
    apply_planes(
        matrix, field, WIDTH, 2 * planes - 2 * WIDTH, nx, y_ref, levels, WIDTH, True,
        store_planes(nx, (first_ref, 0)),
    )


def pass_kernel(after_ref, in_ref, out_ref):
    del after_ref
    out_ref[...] = in_ref[pl.ds(0, out_ref.shape[0]), :]


def add_below(nx, below, factors, base, emit):
    @pl.loop(0, nx)
    def _(x):
        low = [below[aligned((j * nx + x) * GROUP, GROUP), :] for j in range(WIDTH)]
        for i in range(WIDTH):
            total = base[aligned((i * nx + x) * GROUP, GROUP), :]
            for j in range(i, WIDTH):
                total = total + factors[WIDTH + i - j - 1] * low[j]
            emit(i, x, total)


def emit_rows(nx, ref):
    def emit(i, x, value):
        ref[aligned((i * nx + x) * GROUP, GROUP), :] = value

    return emit


def emit_pairs(nx, narrow, ref):
    def emit(i, x, value):
        row = i * nx + x
        pair = jnp.concatenate([narrow[aligned(row * GROUP, GROUP), :], value], axis=0)
        ref[aligned(row * 2 * GROUP, 2 * GROUP), :] = pair.astype(BF16)

    return emit


TWICE_L_FACTORS = tuple(2.0 * c for c in L_FACTORS)


def first_ahead_kernel(
    planes, nx, own_ref, level_ref, early_ref, first_part_ref, beyond_part_ref, values, y_ref,
):
    side = WIDTH * nx * GROUP
    matrix = circulant(y_ref.shape[1])
    values[pl.ds(0, side), :] = jnp.zeros((side, values.shape[1]), F32)
    values[pl.ds(side, 2 * side), :] = own_ref[...]
    apply_planes(
        matrix, values, WIDTH, WIDTH, nx, y_ref, level_ref, 0, True,
        store_planes(nx, (first_part_ref, 0)),
    )
    values[pl.ds(side, 2 * side), :] = early_ref[...]
    apply_planes(
        matrix, values, WIDTH, WIDTH, nx, y_ref, level_ref, WIDTH, True,
        store_second(nx, own_ref, WIDTH, (beyond_part_ref, 0)),
    )


def near_kernel(
    nx, near_ref, first_part_ref, beyond_part_ref, near_field_ref, first_ref, beyond_ref, core_ref
):
    plane_rows = nx * GROUP
    place_planes(near_ref, WIDTH, near_field_ref, WIDTH - 1, -1, plane_rows)
    add_low(near_ref, WIDTH, near_field_ref, WIDTH - 1, plane_rows)
    add_below(nx, near_field_ref, L_FACTORS, first_part_ref, emit_rows(nx, first_ref))
    add_below(nx, first_ref, TWICE_L_FACTORS, beyond_part_ref, emit_rows(nx, beyond_ref))
    core_ref[...] = beyond_ref[...].astype(BF16)


def ahead_kernel(
    planes, nx, own_ref, level_ref, near_ref, near_field_ref, early_ref, first_ref,
    first_part_ref, second_part_ref, values, levels, y_ref,
):
    plane_rows = nx * GROUP
    side = WIDTH * plane_rows
    matrix = circulant(y_ref.shape[1])
    values[pl.ds(0, side), :] = jnp.zeros((side, values.shape[1]), F32)
    values[pl.ds(side, side), :] = near_field_ref[...]
    values[pl.ds(2 * side, side), :] = own_ref[pl.ds(0, side), :]
    place_levels(near_ref, side + plane_rows, WIDTH, nx, levels, WIDTH - 1, 0)
    apply_planes(
        matrix, values, WIDTH, WIDTH, nx, y_ref, levels, 0, True, store_planes(nx, (first_part_ref, 0))
    )
    values[pl.ds(side, side), :] = first_ref[...]
    values[pl.ds(2 * side, side), :] = early_ref[pl.ds(0, side), :]
    apply_planes(
        matrix, values, WIDTH, WIDTH, nx, y_ref, level_ref, 0, True,
        store_second(nx, own_ref, 0, (second_part_ref, 0)),
    )


def right_ahead_kernel(nx, level_ref, beyond_ref, beside_ref, after_ref, right_part_ref, values, y_ref):
    del after_ref
    plane_rows = nx * GROUP
    side = WIDTH * plane_rows
    matrix = circulant(y_ref.shape[1])
    values[pl.ds(0, side), :] = jnp.zeros((side, values.shape[1]), F32)
    values[pl.ds(side, side), :] = beyond_ref[...]
    place_planes(beside_ref, WIDTH, values, 3 * WIDTH - 1, -1, plane_rows)
    apply_planes(
        matrix, values, WIDTH, WIDTH, nx, y_ref, level_ref, WIDTH, False,
        store_planes(nx, (right_part_ref, 0)),
    )


def middle_kernel(
    nx, far_ref, first_part_ref, second_part_ref, first_low_ref, second_ref, below
):
    place_planes(far_ref, WIDTH, below, WIDTH - 1, -1, nx * GROUP)
    add_below(nx, below, L_FACTORS, first_part_ref, emit_rows(nx, first_low_ref))
    add_below(nx, first_low_ref, TWICE_L_FACTORS, second_part_ref, emit_rows(nx, second_ref))


def behind_kernel(
    planes, nx, level_ref, near_ref, near_field_ref, far_ref, first_low_ref, first_ref, second_ref,
    beyond_ref, right_part_ref, first_part_ref, second_part_ref, left_part_ref, right_ref, values, levels, y_ref,
):
    plane_rows = nx * GROUP
    side = WIDTH * plane_rows
    add_below(nx, second_ref, H_FACTORS, right_part_ref, emit_pairs(nx, beyond_ref, right_ref))
    matrix = circulant(y_ref.shape[1])
    values[pl.ds(0, side), :] = jnp.zeros((side, values.shape[1]), F32)
    place_levels(far_ref, side, WIDTH, nx, levels, WIDTH - 1, WIDTH)
    place_levels(near_ref, side + plane_rows, WIDTH, nx, levels, 2 * WIDTH - 1, 0)

    place_planes(far_ref, WIDTH, values, 2 * WIDTH - 1, -1, plane_rows)
    values[pl.ds(2 * side, side), :] = near_field_ref[...]
    apply_planes(
        matrix, values, WIDTH, WIDTH, nx, y_ref, levels, 0, True, store_planes(nx, (first_part_ref, 0))
    )
    values[pl.ds(side, side), :] = first_low_ref[...]
    values[pl.ds(2 * side, side), :] = first_ref[...]
    apply_planes(
        matrix, values, WIDTH, WIDTH, nx, y_ref, levels, WIDTH, True,
        store_second(nx, near_field_ref, 0, (second_part_ref, 0)),
    )
    values[pl.ds(side, side), :] = second_ref[...]
    values[pl.ds(2 * side, side), :] = beyond_ref[...]
    apply_planes(
        matrix, values, WIDTH, WIDTH, nx, y_ref, level_ref, 0, False,
        store_planes(nx, (left_part_ref, 0)),
    )


def left_kernel(
    nx, relay_ref, first_part_ref, second_part_ref, left_part_ref, second_ref, right_ref, out_ref,
    below, lower, pairs,
):
    place_planes(relay_ref, WIDTH, below, 0, 1, nx * GROUP)
    add_below(nx, below, L_FACTORS, first_part_ref, emit_rows(nx, lower))
    add_below(nx, lower, TWICE_L_FACTORS, second_part_ref, emit_rows(nx, below))
    add_below(nx, below, H_FACTORS, left_part_ref, emit_pairs(nx, second_ref, pairs))
    band, height, _ = out_ref.shape
    me = lax.axis_index("band")
    for i in range(band // 2):
        at = pl.ds(i * height, height)
        out_ref[i ^ me] = pairs[at, :]
        out_ref[(band // 2 + i) ^ me] = right_ref[at, :]


def write_kernel(planes, nx, second_ref, beyond_ref, filtered_ref, done_ref):
    done_ref[...] = jnp.zeros_like(done_ref)
    rows = planes * nx
    odd = lax.rem(lax.axis_index("space"), 2)
    for ref, first in ((second_ref, 0), (beyond_ref, WIDTH)):

        @pl.loop(0, WIDTH)
        def _(i):
            plane = first + i
            target = lax.select(odd == 1, planes - 1 - plane, plane) * nx
            for x in range(nx):
                value = ref[aligned((i * nx + x) * GROUP, GROUP), :]
                filtered_ref[pl.ds(target + x, GROUP, stride=rows), :] = value


def gram_kernel(space, steps, order, *refs):
    after_ref, *blocks, out_ref, held = refs
    del after_ref
    band = len(blocks)
    width = 2 * GROUP
    me = lax.axis_index("band")
    for k, block in zip(order, blocks):
        held[k ^ me] = block[...]
    total = jnp.zeros((band * width, band * width), F32)
    for step in range(0, steps, 2):
        block = jnp.concatenate(
            [held[:, pl.ds((step + i) * width, width), :].reshape(band * width, -1) for i in range(2)],
            axis=1,
        )
        total = total + lax.dot_general(
            block, block, (((1,), (1,)), ((), ())), preferred_element_type=F32
        )
    lanes = lax.broadcasted_iota(jnp.int32, (GROUP, band * width), 1)
    for b in range(band):
        narrow = total[b * width : b * width + GROUP]
        applied = pltpu.roll(total[b * width + GROUP : (b + 1) * width], GROUP, 1)
        piece = jnp.where(lanes % width < GROUP, narrow, applied)
        for s in range(space):
            out_ref[s * band + b] = piece


def sum_kernel(scale, in_ref, intersection_ref, projected_ref):
    total = in_ref[0]
    for i in range(1, in_ref.shape[0]):
        total = total + in_ref[i]
    total = total * scale
    lanes, columns = total.shape[1], intersection_ref.shape[1]
    source = lax.broadcasted_iota(jnp.int32, (lanes, columns), 0)
    target = lax.broadcasted_iota(jnp.int32, (lanes, columns), 1)
    place = (target // GROUP) * (2 * GROUP) + target % GROUP
    for offset, ref in ((0, intersection_ref), (GROUP, projected_ref)):
        pick = jnp.where(source == place + offset, 1.0, 0.0).astype(F32)
        ref[...] = jnp.dot(total, pick, precision=lax.Precision.HIGHEST, preferred_element_type=F32)


ORDER = (1, 2, 4, 6, 5, 7, 3)


def call(kernel, outs, *args, scratch=(), hbm_in=0, hbm_out=(), vmem=40, flops=1000000):
    anywhere = pl.BlockSpec(memory_space=pl.ANY)
    return pl.pallas_call(
        kernel,
        out_shape=outs,
        in_specs=[anywhere] * hbm_in + [VMEM] * (len(args) - hbm_in),
        out_specs=tuple(anywhere if i in hbm_out else VMEM for i in range(len(outs))),
        scratch_shapes=list(scratch),
        compiler_params=pltpu.CompilerParams(vmem_limit_bytes=int(vmem * 2**20)),
        cost_estimate=pl.CostEstimate(flops=flops, bytes_accessed=1000000, transcendentals=0),
    )(*args)


def shifts(axis):
    count = lax.axis_size(axis)
    up = [(i, (i + 1) % count) for i in range(count)]
    return up, [(j, i) for i, j in up]


def local_kernels(orbitals, potential):
    count, planes, nx, ny = orbitals.shape
    space, band = lax.axis_size("space"), lax.axis_size("band")
    rows = planes * nx
    plane_rows = nx * GROUP
    size = planes * plane_rows
    struct = jax.ShapeDtypeStruct
    other_core = [(i, i ^ 1) for i in range(space)]
    other_chip = [(i, i ^ 3) for i in range(space)]

    def f32_planes(many, height=plane_rows):
        return pltpu.VMEM((many * height, ny), F32)

    def bf16_rows(height):
        return struct((height, ny), BF16)

    half = WIDTH * plane_rows
    slab, half_slab = struct((size, ny), F32), struct((half, ny), F32)
    parts = 4
    own, levels, to_near, to_far, to_core = call(
        functools.partial(prepare_kernel, planes, nx),
        (
            slab,
            struct((rows, ny), F32),
            bf16_rows(half + plane_rows + (WIDTH + NEAR) * nx),
            bf16_rows(half + WIDTH * nx),
            bf16_rows(size + plane_rows + (planes + NEAR) * nx),
        ),
        orbitals, potential.reshape(rows, ny),
        hbm_in=2, vmem=52,
        scratch=[
            pltpu.VMEM(orbitals.shape, F32),
            pltpu.VMEM((rows, ny), F32),
            pltpu.SemaphoreType.DMA((parts + 1,)),
        ],
    )
    near = lax.ppermute(to_near, "space", other_chip)
    core = lax.ppermute(to_core, "space", other_core)
    far = lax.ppermute(to_far, "space", other_chip)
    (early,) = call(
        functools.partial(early_kernel, planes, nx),
        (slab,),
        own, levels, core,
        scratch=[f32_planes(2 * planes), f32_planes(2 * planes, nx), f32_planes(planes)],
    )
    wide = planes + WIDTH
    part = [f32_planes(wide), f32_planes(planes, nx), f32_planes(WIDTH)]
    first_part, beyond_part = call(
        functools.partial(first_ahead_kernel, planes, nx),
        (half_slab,) * 2,
        own, levels, early,
        scratch=[part[0], part[2]],
    )
    near_field, first, beyond, to_beside = call(
        functools.partial(near_kernel, nx),
        (half_slab,) * 3 + (bf16_rows(half),),
        near, first_part, beyond_part,
    )
    beside = lax.ppermute(to_beside, "space", other_core)
    first_part, second_part = call(
        functools.partial(ahead_kernel, planes, nx),
        (half_slab,) * 2,
        own, levels, near, near_field, early, first,
        scratch=part,
    )
    (right_part,) = call(
        functools.partial(right_ahead_kernel, nx),
        (half_slab,),
        levels, beyond, beside, first_part,
        scratch=[part[0], part[2]],
    )
    (relay,) = call(pass_kernel, (bf16_rows(half),), right_part, far, hbm_in=1)
    relay = lax.ppermute(relay, "space", other_core)
    first_low, second = call(
        functools.partial(middle_kernel, nx),
        (half_slab,) * 2,
        far, first_part, second_part,
        scratch=[f32_planes(WIDTH)],
    )
    first_part, second_part, left_part, right = call(
        functools.partial(behind_kernel, planes, nx),
        (half_slab,) * 3 + (bf16_rows(2 * half),),
        levels, near, near_field, far, first_low, first, second, beyond, right_part,
        scratch=part,
    )
    steps = rows // band
    block = (steps * 2 * GROUP, ny)
    (pairs,) = call(
        functools.partial(left_kernel, nx),
        (struct((band, *block), BF16),),
        relay, first_part, second_part, left_part, second, right,
        scratch=[f32_planes(WIDTH), f32_planes(WIDTH), pltpu.VMEM((2 * half, ny), BF16)],
    )
    filtered, written = call(
        functools.partial(write_kernel, planes, nx),
        (struct((count * rows, ny), F32), struct((GROUP, ny), F32)),
        second, beyond,
    )
    order = (0,) + ORDER[::-1]
    blocks = [
        lax.ppermute(pairs[k], "band", [(i, i ^ k) for i in range(band)]) if k else pairs[k]
        for k in order
    ]
    (pieces,) = call(
        functools.partial(gram_kernel, space, steps, order),
        (struct((space * band, GROUP, band * 2 * GROUP), F32),),
        written, *blocks,
        hbm_in=1,
        scratch=[pltpu.VMEM((band, *block), BF16)],
    )
    pieces = lax.all_to_all(pieces, ("space", "band"), 0, 0, tiled=True)
    rows_out = struct((count, count * band), F32)
    intersection, projected = call(
        functools.partial(sum_kernel, 1.0 / (rows * ny * space)), (rows_out, rows_out), pieces
    )
    return filtered.reshape(orbitals.shape), intersection, projected


def padded(cells, width):
    up, down = shifts("space")
    head, tail = cells[:, :width], cells[:, cells.shape[1] - width :]
    return jnp.concatenate(
        [lax.ppermute(tail, "space", up), cells, lax.ppermute(head, "space", down)], axis=1
    )


def hamiltonian(beside, potential):
    planes = beside.shape[1] - 2 * WIDTH
    center = beside[:, WIDTH : WIDTH + planes]
    summed = 3.0 * STENCIL[0] * center
    for k in range(1, WIDTH + 1):
        near = beside[:, WIDTH + k : WIDTH + k + planes] + beside[:, WIDTH - k : WIDTH - k + planes]
        for dim in (2, 3):
            near = near + (jnp.roll(center, k, dim) + jnp.roll(center, -k, dim))
        summed = summed + STENCIL[k] * near
    return -0.5 * summed + potential * center


def local_plain(orbitals, potential):
    def step(field):
        return (hamiltonian(padded(field, WIDTH), potential) - 9.0 * field) * 0.125

    filtered = 2.0 * step(step(orbitals)) - orbitals
    beside = padded(filtered.astype(BF16), WIDTH).astype(F32)
    applied = hamiltonian(beside, potential).astype(BF16)
    count = orbitals.shape[0]
    narrow = filtered.astype(BF16).reshape(count, -1)
    applied = applied.reshape(count, -1)
    everyone = lax.all_gather(narrow, "band", axis=0, tiled=True)
    contract = (((1,), (1,)), ((), ()))
    parts = [
        lax.dot_general(rows, everyone, contract, preferred_element_type=F32)
        for rows in (narrow, applied)
    ]
    scale = 1.0 / (narrow.shape[1] * lax.axis_size("space"))
    intersection, projected = lax.psum(tuple(parts), "space")
    return filtered, intersection * scale, projected * scale


def local(orbitals, potential):
    count, planes, nx, ny = orbitals.shape
    band = lax.axis_size("band")
    fits = (
        count == GROUP
        and lax.axis_size("space") == 4
        and planes == 2 * WIDTH
        and nx == 16
        and ny == 128
        and band * 2 * GROUP == 128
        and (planes * nx) % (2 * band) == 0
    )
    return (local_kernels if fits else local_plain)(orbitals, potential)


def solution(mesh):
    return jax.shard_map(
        local,
        mesh=mesh,
        in_specs=(P("band", "space", None, None), P("space", None, None)),
        out_specs=(P("band", "space", None, None), P("band", None), P("band", None)),
        check_vma=False,
    )
```

```python
import functools

import jax
import jax.numpy as jnp
from jax import lax
from jax.experimental import pallas as pl
from jax.experimental.pallas import tpu as pltpu
from jax.sharding import PartitionSpec as P

STENCIL = (
    -5369.0 / 1800.0,
    12.0 / 7.0,
    -15.0 / 56.0,
    10.0 / 189.0,
    -1.0 / 112.0,
    2.0 / 1925.0,
    -1.0 / 16632.0,
)
WIDTH = 6
BF16 = jnp.bfloat16
F32 = jnp.float32
VMEM = pl.BlockSpec(memory_space=pltpu.VMEM)

GROUP = 8

H_FACTORS = tuple(-0.5 * c for c in STENCIL[1:])
H_CENTER = -1.5 * STENCIL[0]
L_FACTORS = tuple(0.125 * c for c in H_FACTORS)
L_CENTER = (H_CENTER - 9.0) / 8.0


def aligned(start, size):
    return pl.ds(pl.multiple_of(start, size), size)


def low_part(block):
    return block - block.astype(BF16).astype(F32)


def circulant(ny):
    row = lax.broadcasted_iota(jnp.int32, (ny, ny), 0)
    column = lax.broadcasted_iota(jnp.int32, (ny, ny), 1)
    apart = jnp.abs(row - column)
    apart = jnp.minimum(apart, ny - apart)
    matrix = jnp.zeros((ny, ny), F32)
    for k in range(1, WIDTH + 1):
        matrix = jnp.where(apart == k, H_FACTORS[k - 1] / H_FACTORS[0], matrix)
    matrix = matrix.astype(BF16)
    return jnp.concatenate([matrix, matrix], axis=0)


def along_y(matrix, source, start, count, y_ref, plane_rows):
    step = min(count, WIDTH)
    for i in range(0, count, step):
        block = source[pl.ds((start + i) * plane_rows, step * plane_rows), :]
        parts = jnp.concatenate([block.astype(BF16), low_part(block).astype(BF16)], axis=1)
        y_ref[pl.ds(i * plane_rows, step * plane_rows), :] = jnp.dot(
            parts, matrix, preferred_element_type=F32
        )


def apply_planes(matrix, source, start, count, nx, y_ref, levels, level, linear, emit):
    plane_rows = nx * GROUP
    along_y(matrix, source, start, count, y_ref, plane_rows)
    factors = L_FACTORS if linear else H_FACTORS

    def load(row):
        return source[aligned(row, GROUP), :]

    @pl.loop(0, count)
    def _(i):
        where = (start + i) * plane_rows
        center = [load(where + x * GROUP) for x in range(nx)]
        values = [None] * nx
        half = nx // 2
        for x in range(half):
            shared = {k: center[(x + k) % nx] + center[(x - k) % nx] for k in range(1, half)}
            for at in (x, x + half):
                row = levels[pl.ds((level + i) * nx + at, 1), :]
                row = 0.125 * row + L_CENTER if linear else row + H_CENTER
                total = jnp.broadcast_to(row, center[at].shape) * center[at]
                total = total + factors[0] * y_ref[aligned(i * plane_rows + at * GROUP, GROUP), :]
                for k in range(1, WIDTH + 1):
                    up, down = where + k * plane_rows + at * GROUP, where - k * plane_rows + at * GROUP
                    near = load(up) + load(down) + shared[k if at == x else half - k]
                    total = total + factors[k - 1] * near
                values[at] = total
        emit(i, values, center)


def own_kernel(planes, nx, orbitals_hbm, own_ref, orbitals, semaphores):
    rows = planes * nx
    parts = semaphores.shape[0]
    each = planes // parts
    odd = lax.rem(lax.axis_index("space"), 2)

    def fetch(i):
        at = pl.ds(i * each, each)
        return pltpu.make_async_copy(orbitals_hbm.at[:, at], orbitals.at[:, at], semaphores.at[i])

    for i in range(parts):
        fetch(i).start()
    cells = orbitals.reshape(GROUP * rows, orbitals.shape[-1])
    for i in range(parts):
        fetch(i).wait()

        @pl.loop(i * each, (i + 1) * each)
        def _(plane):
            target = lax.select(odd == 1, planes - 1 - plane, plane) * nx
            for x in range(nx):
                value = cells[pl.ds(plane * nx + x, GROUP, stride=rows), :]
                own_ref[aligned((target + x) * GROUP, GROUP), :] = value


def messages_kernel(planes, nx, own_ref, potential_ref, level_ref, near_ref, far_ref, core_ref):
    plane_rows = nx * GROUP
    side, size = WIDTH * plane_rows, planes * plane_rows
    odd = lax.rem(lax.axis_index("space"), 2)
    for start, ref in ((0, near_ref), (side, far_ref)):
        high = own_ref[pl.ds(start, side), :].astype(BF16)
        ref[pl.ds(0, side), :] = high
        core_ref[pl.ds(start, side), :] = high
    for out_ref, plane, at in ((near_ref, 0, side), (core_ref, planes - 1, size)):
        block = own_ref[pl.ds(plane * plane_rows, plane_rows), :]
        out_ref[pl.ds(at, plane_rows), :] = low_part(block).astype(BF16)
    for plane in range(planes):
        source = lax.select(odd == 1, planes - 1 - plane, plane) * nx
        block = potential_ref[aligned(source, nx), :]
        level_ref[pl.ds(plane * nx, nx), :] = block
        core_ref[pl.ds(size + plane_rows + plane * nx, nx), :] = block.astype(BF16)
        if plane < WIDTH:
            near_ref[pl.ds(side + plane_rows + plane * nx, nx), :] = block.astype(BF16)
        else:
            far_ref[pl.ds(side + (plane - WIDTH) * nx, nx), :] = block.astype(BF16)
        if plane < NEAR:
            at = side + plane_rows + (WIDTH + plane) * nx
            near_ref[pl.ds(at, nx), :] = low_part(block).astype(BF16)
        if plane >= planes - NEAR:
            at = size + plane_rows + (planes + plane - (planes - NEAR)) * nx
            core_ref[pl.ds(at, nx), :] = low_part(block).astype(BF16)


NEAR = 2


def place_planes(message, count, field, where, step, plane_rows):
    for i in range(count):
        block = message[pl.ds(i * plane_rows, plane_rows), :]
        field[pl.ds((where + step * i) * plane_rows, plane_rows), :] = block.astype(F32)


def add_low(message, planes, field, where, plane_rows):
    at = pl.ds(where * plane_rows, plane_rows)
    field[at, :] = field[at, :] + message[pl.ds(planes * plane_rows, plane_rows), :].astype(F32)


def place_levels(message, extra, count, nx, levels, where, near):
    for i in range(count):
        block = message[pl.ds(extra + i * nx, nx), :].astype(F32)
        if near <= i < near + NEAR:
            block = block + message[pl.ds(extra + (count + i - near) * nx, nx), :].astype(F32)
        levels[pl.ds((where - i) * nx, nx), :] = block


def store_planes(nx, *refs):
    def emit(i, values, center):
        for x in range(nx):
            for ref, first in refs:
                ref[aligned(((first + i) * nx + x) * GROUP, GROUP), :] = values[x]

    return emit


def store_second(nx, before, start, *refs):
    def emit(i, values, center):
        for x in range(nx):
            row = (i * nx + x) * GROUP
            value = 2.0 * values[x] - before[aligned(start * nx * GROUP + row, GROUP), :]
            for ref, first in refs:
                ref[aligned(first * nx * GROUP + row, GROUP), :] = value

    return emit


def early_kernel(planes, nx, own_ref, level_ref, core_ref, first_ref, field, levels, y_ref):
    plane_rows = nx * GROUP
    field[pl.ds(0, planes * plane_rows), :] = own_ref[...]
    place_planes(core_ref, planes, field, 2 * planes - 1, -1, plane_rows)
    add_low(core_ref, planes, field, planes, plane_rows)
    levels[pl.ds(0, planes * nx), :] = level_ref[...]
    extra = (planes + 1) * plane_rows
    place_levels(core_ref, extra, planes, nx, levels, 2 * planes - 1, planes - NEAR)
    matrix = circulant(y_ref.shape[1])
    apply_planes(
        matrix, field, WIDTH, 2 * planes - 2 * WIDTH, nx, y_ref, levels, WIDTH, True,
        store_planes(nx, (first_ref, 0)),
    )


def pass_kernel(after_ref, in_ref, out_ref):
    del after_ref
    out_ref[...] = in_ref[pl.ds(0, out_ref.shape[0]), :]


def add_below(nx, below, factors, base, emit):
    @pl.loop(0, nx)
    def _(x):
        low = [below[aligned((j * nx + x) * GROUP, GROUP), :] for j in range(WIDTH)]
        for i in range(WIDTH):
            total = base[aligned((i * nx + x) * GROUP, GROUP), :]
            for j in range(i, WIDTH):
                total = total + factors[WIDTH + i - j - 1] * low[j]
            emit(i, x, total)


def emit_rows(nx, ref):
    def emit(i, x, value):
        ref[aligned((i * nx + x) * GROUP, GROUP), :] = value

    return emit


def emit_pairs(nx, narrow, ref):
    def emit(i, x, value):
        row = i * nx + x
        pair = jnp.concatenate([narrow[aligned(row * GROUP, GROUP), :], value], axis=0)
        ref[aligned(row * 2 * GROUP, 2 * GROUP), :] = pair.astype(BF16)

    return emit


TWICE_L_FACTORS = tuple(2.0 * c for c in L_FACTORS)


def first_ahead_kernel(
    planes, nx, own_ref, level_ref, early_ref, first_part_ref, beyond_part_ref, values, y_ref,
):
    side = WIDTH * nx * GROUP
    matrix = circulant(y_ref.shape[1])
    values[pl.ds(0, side), :] = jnp.zeros((side, values.shape[1]), F32)
    values[pl.ds(side, 2 * side), :] = own_ref[...]
    apply_planes(
        matrix, values, WIDTH, WIDTH, nx, y_ref, level_ref, 0, True,
        store_planes(nx, (first_part_ref, 0)),
    )
    values[pl.ds(side, 2 * side), :] = early_ref[...]
    apply_planes(
        matrix, values, WIDTH, WIDTH, nx, y_ref, level_ref, WIDTH, True,
        store_second(nx, own_ref, WIDTH, (beyond_part_ref, 0)),
    )


def near_kernel(
    nx, near_ref, first_part_ref, beyond_part_ref, near_field_ref, first_ref, beyond_ref, core_ref
):
    plane_rows = nx * GROUP
    place_planes(near_ref, WIDTH, near_field_ref, WIDTH - 1, -1, plane_rows)
    add_low(near_ref, WIDTH, near_field_ref, WIDTH - 1, plane_rows)
    add_below(nx, near_field_ref, L_FACTORS, first_part_ref, emit_rows(nx, first_ref))
    add_below(nx, first_ref, TWICE_L_FACTORS, beyond_part_ref, emit_rows(nx, beyond_ref))
    core_ref[...] = beyond_ref[...].astype(BF16)


def ahead_kernel(
    planes, nx, own_ref, level_ref, near_ref, near_field_ref, early_ref, first_ref,
    first_part_ref, second_part_ref, values, levels, y_ref,
):
    plane_rows = nx * GROUP
    side = WIDTH * plane_rows
    matrix = circulant(y_ref.shape[1])
    values[pl.ds(0, side), :] = jnp.zeros((side, values.shape[1]), F32)
    values[pl.ds(side, side), :] = near_field_ref[...]
    values[pl.ds(2 * side, side), :] = own_ref[pl.ds(0, side), :]
    place_levels(near_ref, side + plane_rows, WIDTH, nx, levels, WIDTH - 1, 0)
    apply_planes(
        matrix, values, WIDTH, WIDTH, nx, y_ref, levels, 0, True, store_planes(nx, (first_part_ref, 0))
    )
    values[pl.ds(side, side), :] = first_ref[...]
    values[pl.ds(2 * side, side), :] = early_ref[pl.ds(0, side), :]
    apply_planes(
        matrix, values, WIDTH, WIDTH, nx, y_ref, level_ref, 0, True,
        store_second(nx, own_ref, 0, (second_part_ref, 0)),
    )


def right_ahead_kernel(nx, level_ref, beyond_ref, beside_ref, after_ref, right_part_ref, values, y_ref):
    del after_ref
    plane_rows = nx * GROUP
    side = WIDTH * plane_rows
    matrix = circulant(y_ref.shape[1])
    values[pl.ds(0, side), :] = jnp.zeros((side, values.shape[1]), F32)
    values[pl.ds(side, side), :] = beyond_ref[...]
    place_planes(beside_ref, WIDTH, values, 3 * WIDTH - 1, -1, plane_rows)
    apply_planes(
        matrix, values, WIDTH, WIDTH, nx, y_ref, level_ref, WIDTH, False,
        store_planes(nx, (right_part_ref, 0)),
    )


def middle_kernel(
    nx, far_ref, first_part_ref, second_part_ref, first_low_ref, second_ref, below
):
    place_planes(far_ref, WIDTH, below, WIDTH - 1, -1, nx * GROUP)
    add_below(nx, below, L_FACTORS, first_part_ref, emit_rows(nx, first_low_ref))
    add_below(nx, first_low_ref, TWICE_L_FACTORS, second_part_ref, emit_rows(nx, second_ref))


def behind_kernel(
    planes, nx, level_ref, near_ref, near_field_ref, far_ref, first_low_ref, first_ref, second_ref,
    beyond_ref, right_part_ref, first_part_ref, second_part_ref, left_part_ref, right_ref, values, levels, y_ref,
):
    plane_rows = nx * GROUP
    side = WIDTH * plane_rows
    add_below(nx, second_ref, H_FACTORS, right_part_ref, emit_pairs(nx, beyond_ref, right_ref))
    matrix = circulant(y_ref.shape[1])
    values[pl.ds(0, side), :] = jnp.zeros((side, values.shape[1]), F32)
    place_levels(far_ref, side, WIDTH, nx, levels, WIDTH - 1, WIDTH)
    place_levels(near_ref, side + plane_rows, WIDTH, nx, levels, 2 * WIDTH - 1, 0)

    place_planes(far_ref, WIDTH, values, 2 * WIDTH - 1, -1, plane_rows)
    values[pl.ds(2 * side, side), :] = near_field_ref[...]
    apply_planes(
        matrix, values, WIDTH, WIDTH, nx, y_ref, levels, 0, True, store_planes(nx, (first_part_ref, 0))
    )
    values[pl.ds(side, side), :] = first_low_ref[...]
    values[pl.ds(2 * side, side), :] = first_ref[...]
    apply_planes(
        matrix, values, WIDTH, WIDTH, nx, y_ref, levels, WIDTH, True,
        store_second(nx, near_field_ref, 0, (second_part_ref, 0)),
    )
    values[pl.ds(side, side), :] = second_ref[...]
    values[pl.ds(2 * side, side), :] = beyond_ref[...]
    apply_planes(
        matrix, values, WIDTH, WIDTH, nx, y_ref, level_ref, 0, False,
        store_planes(nx, (left_part_ref, 0)),
    )


def left_kernel(
    nx, relay_ref, first_part_ref, second_part_ref, left_part_ref, second_ref, right_ref, out_ref,
    below, lower, pairs,
):
    place_planes(relay_ref, WIDTH, below, 0, 1, nx * GROUP)
    add_below(nx, below, L_FACTORS, first_part_ref, emit_rows(nx, lower))
    add_below(nx, lower, TWICE_L_FACTORS, second_part_ref, emit_rows(nx, below))
    add_below(nx, below, H_FACTORS, left_part_ref, emit_pairs(nx, second_ref, pairs))
    band, height, _ = out_ref.shape
    me = lax.axis_index("band")
    for i in range(band // 2):
        at = pl.ds(i * height, height)
        out_ref[i ^ me] = pairs[at, :]
        out_ref[(band // 2 + i) ^ me] = right_ref[at, :]


def write_kernel(planes, nx, second_ref, beyond_ref, filtered_ref, done_ref):
    done_ref[...] = jnp.zeros_like(done_ref)
    rows = planes * nx
    odd = lax.rem(lax.axis_index("space"), 2)
    for ref, first in ((second_ref, 0), (beyond_ref, WIDTH)):

        @pl.loop(0, WIDTH)
        def _(i):
            plane = first + i
            target = lax.select(odd == 1, planes - 1 - plane, plane) * nx
            for x in range(nx):
                value = ref[aligned((i * nx + x) * GROUP, GROUP), :]
                filtered_ref[pl.ds(target + x, GROUP, stride=rows), :] = value


def gram_kernel(space, steps, order, *refs):
    after_ref, *blocks, out_ref, held = refs
    del after_ref
    band = len(blocks)
    width = 2 * GROUP
    me = lax.axis_index("band")
    for k, block in zip(order, blocks):
        held[k ^ me] = block[...]
    total = jnp.zeros((band * width, band * width), F32)
    for step in range(0, steps, 2):
        block = jnp.concatenate(
            [held[:, pl.ds((step + i) * width, width), :].reshape(band * width, -1) for i in range(2)],
            axis=1,
        )
        total = total + lax.dot_general(
            block, block, (((1,), (1,)), ((), ())), preferred_element_type=F32
        )
    lanes = lax.broadcasted_iota(jnp.int32, (GROUP, band * width), 1)
    for b in range(band):
        narrow = total[b * width : b * width + GROUP]
        applied = pltpu.roll(total[b * width + GROUP : (b + 1) * width], GROUP, 1)
        piece = jnp.where(lanes % width < GROUP, narrow, applied)
        for s in range(space):
            out_ref[s * band + b] = piece


def sum_kernel(scale, in_ref, intersection_ref, projected_ref):
    total = in_ref[0]
    for i in range(1, in_ref.shape[0]):
        total = total + in_ref[i]
    total = total * scale
    lanes, columns = total.shape[1], intersection_ref.shape[1]
    source = lax.broadcasted_iota(jnp.int32, (lanes, columns), 0)
    target = lax.broadcasted_iota(jnp.int32, (lanes, columns), 1)
    place = (target // GROUP) * (2 * GROUP) + target % GROUP
    for offset, ref in ((0, intersection_ref), (GROUP, projected_ref)):
        pick = jnp.where(source == place + offset, 1.0, 0.0).astype(F32)
        ref[...] = jnp.dot(total, pick, precision=lax.Precision.HIGHEST, preferred_element_type=F32)


VMEM_FIRST = 53

ORDER = (1, 2, 4, 6, 5, 7, 3)


def call(kernel, outs, *args, scratch=(), hbm_in=0, hbm_out=(), vmem=40, flops=1000000):
    anywhere = pl.BlockSpec(memory_space=pl.ANY)
    return pl.pallas_call(
        kernel,
        out_shape=outs,
        in_specs=[anywhere] * hbm_in + [VMEM] * (len(args) - hbm_in),
        out_specs=tuple(anywhere if i in hbm_out else VMEM for i in range(len(outs))),
        scratch_shapes=list(scratch),
        compiler_params=pltpu.CompilerParams(vmem_limit_bytes=int(vmem * 2**20)),
        cost_estimate=pl.CostEstimate(flops=flops, bytes_accessed=1000000, transcendentals=0),
    )(*args)


def shifts(axis):
    count = lax.axis_size(axis)
    up = [(i, (i + 1) % count) for i in range(count)]
    return up, [(j, i) for i, j in up]


def local_kernels(orbitals, potential):
    count, planes, nx, ny = orbitals.shape
    space, band = lax.axis_size("space"), lax.axis_size("band")
    rows = planes * nx
    plane_rows = nx * GROUP
    size = planes * plane_rows
    struct = jax.ShapeDtypeStruct
    other_core = [(i, i ^ 1) for i in range(space)]
    other_chip = [(i, i ^ 3) for i in range(space)]

    def f32_planes(many, height=plane_rows):
        return pltpu.VMEM((many * height, ny), F32)

    def bf16_rows(height):
        return struct((height, ny), BF16)

    half = WIDTH * plane_rows
    slab, half_slab = struct((size, ny), F32), struct((half, ny), F32)
    (own,) = call(
        functools.partial(own_kernel, planes, nx),
        (slab,),
        orbitals,
        hbm_in=1, vmem=VMEM_FIRST,
        scratch=[pltpu.VMEM(orbitals.shape, F32), pltpu.SemaphoreType.DMA((4,))],
    )
    levels, to_near, to_far, to_core = call(
        functools.partial(messages_kernel, planes, nx),
        (
            struct((rows, ny), F32),
            bf16_rows(half + plane_rows + (WIDTH + NEAR) * nx),
            bf16_rows(half + WIDTH * nx),
            bf16_rows(size + plane_rows + (planes + NEAR) * nx),
        ),
        own, potential.reshape(rows, ny),
    )
    near = lax.ppermute(to_near, "space", other_chip)
    core = lax.ppermute(to_core, "space", other_core)
    far = lax.ppermute(to_far, "space", other_chip)
    (early,) = call(
        functools.partial(early_kernel, planes, nx),
        (slab,),
        own, levels, core,
        scratch=[f32_planes(2 * planes), f32_planes(2 * planes, nx), f32_planes(planes)],
    )
    wide = planes + WIDTH
    part = [f32_planes(wide), f32_planes(planes, nx), f32_planes(WIDTH)]
    first_part, beyond_part = call(
        functools.partial(first_ahead_kernel, planes, nx),
        (half_slab,) * 2,
        own, levels, early,
        scratch=[part[0], part[2]],
    )
    near_field, first, beyond, to_beside = call(
        functools.partial(near_kernel, nx),
        (half_slab,) * 3 + (bf16_rows(half),),
        near, first_part, beyond_part,
    )
    beside = lax.ppermute(to_beside, "space", other_core)
    first_part, second_part = call(
        functools.partial(ahead_kernel, planes, nx),
        (half_slab,) * 2,
        own, levels, near, near_field, early, first,
        scratch=part,
    )
    (right_part,) = call(
        functools.partial(right_ahead_kernel, nx),
        (half_slab,),
        levels, beyond, beside, first_part,
        scratch=[part[0], part[2]],
    )
    (relay,) = call(pass_kernel, (bf16_rows(half),), right_part, far, hbm_in=1)
    relay = lax.ppermute(relay, "space", other_core)
    first_low, second = call(
        functools.partial(middle_kernel, nx),
        (half_slab,) * 2,
        far, first_part, second_part,
        scratch=[f32_planes(WIDTH)],
    )
    first_part, second_part, left_part, right = call(
        functools.partial(behind_kernel, planes, nx),
        (half_slab,) * 3 + (bf16_rows(2 * half),),
        levels, near, near_field, far, first_low, first, second, beyond, right_part,
        scratch=part,
    )
    steps = rows // band
    block = (steps * 2 * GROUP, ny)
    (pairs,) = call(
        functools.partial(left_kernel, nx),
        (struct((band, *block), BF16),),
        relay, first_part, second_part, left_part, second, right,
        scratch=[f32_planes(WIDTH), f32_planes(WIDTH), pltpu.VMEM((2 * half, ny), BF16)],
    )
    filtered, written = call(
        functools.partial(write_kernel, planes, nx),
        (struct((count * rows, ny), F32), struct((GROUP, ny), F32)),
        second, beyond,
    )
    order = (0,) + ORDER[::-1]
    blocks = [
        lax.ppermute(pairs[k], "band", [(i, i ^ k) for i in range(band)]) if k else pairs[k]
        for k in order
    ]
    (pieces,) = call(
        functools.partial(gram_kernel, space, steps, order),
        (struct((space * band, GROUP, band * 2 * GROUP), F32),),
        written, *blocks,
        hbm_in=1,
        scratch=[pltpu.VMEM((band, *block), BF16)],
    )
    pieces = lax.all_to_all(pieces, ("space", "band"), 0, 0, tiled=True)
    rows_out = struct((count, count * band), F32)
    intersection, projected = call(
        functools.partial(sum_kernel, 1.0 / (rows * ny * space)), (rows_out, rows_out), pieces
    )
    return filtered.reshape(orbitals.shape), intersection, projected


def padded(cells, width):
    up, down = shifts("space")
    head, tail = cells[:, :width], cells[:, cells.shape[1] - width :]
    return jnp.concatenate(
        [lax.ppermute(tail, "space", up), cells, lax.ppermute(head, "space", down)], axis=1
    )


def hamiltonian(beside, potential):
    planes = beside.shape[1] - 2 * WIDTH
    center = beside[:, WIDTH : WIDTH + planes]
    summed = 3.0 * STENCIL[0] * center
    for k in range(1, WIDTH + 1):
        near = beside[:, WIDTH + k : WIDTH + k + planes] + beside[:, WIDTH - k : WIDTH - k + planes]
        for dim in (2, 3):
            near = near + (jnp.roll(center, k, dim) + jnp.roll(center, -k, dim))
        summed = summed + STENCIL[k] * near
    return -0.5 * summed + potential * center


def local_plain(orbitals, potential):
    def step(field):
        return (hamiltonian(padded(field, WIDTH), potential) - 9.0 * field) * 0.125

    filtered = 2.0 * step(step(orbitals)) - orbitals
    beside = padded(filtered.astype(BF16), WIDTH).astype(F32)
    applied = hamiltonian(beside, potential).astype(BF16)
    count = orbitals.shape[0]
    narrow = filtered.astype(BF16).reshape(count, -1)
    applied = applied.reshape(count, -1)
    everyone = lax.all_gather(narrow, "band", axis=0, tiled=True)
    contract = (((1,), (1,)), ((), ()))
    parts = [
        lax.dot_general(rows, everyone, contract, preferred_element_type=F32)
        for rows in (narrow, applied)
    ]
    scale = 1.0 / (narrow.shape[1] * lax.axis_size("space"))
    intersection, projected = lax.psum(tuple(parts), "space")
    return filtered, intersection * scale, projected * scale


def local(orbitals, potential):
    count, planes, nx, ny = orbitals.shape
    band = lax.axis_size("band")
    fits = (
        count == GROUP
        and lax.axis_size("space") == 4
        and planes == 2 * WIDTH
        and nx == 16
        and ny == 128
        and band * 2 * GROUP == 128
        and (planes * nx) % (2 * band) == 0
    )
    return (local_kernels if fits else local_plain)(orbitals, potential)


def solution(mesh):
    return jax.shard_map(
        local,
        mesh=mesh,
        in_specs=(P("band", "space", None, None), P("space", None, None)),
        out_specs=(P("band", "space", None, None), P("band", None), P("band", None)),
        check_vma=False,
    )
```

```python
import functools

import jax
import jax.numpy as jnp
from jax import lax
from jax.experimental import pallas as pl
from jax.experimental.pallas import tpu as pltpu
from jax.sharding import PartitionSpec as P

STENCIL = (
    -5369.0 / 1800.0,
    12.0 / 7.0,
    -15.0 / 56.0,
    10.0 / 189.0,
    -1.0 / 112.0,
    2.0 / 1925.0,
    -1.0 / 16632.0,
)
WIDTH = 6
BF16 = jnp.bfloat16
F32 = jnp.float32
VMEM = pl.BlockSpec(memory_space=pltpu.VMEM)

GROUP = 8

H_FACTORS = tuple(-0.5 * c for c in STENCIL[1:])
H_CENTER = -1.5 * STENCIL[0]
L_FACTORS = tuple(0.125 * c for c in H_FACTORS)
L_CENTER = (H_CENTER - 9.0) / 8.0


def aligned(start, size):
    return pl.ds(pl.multiple_of(start, size), size)


def low_part(block):
    return block - block.astype(BF16).astype(F32)


def circulant(ny):
    row = lax.broadcasted_iota(jnp.int32, (ny, ny), 0)
    column = lax.broadcasted_iota(jnp.int32, (ny, ny), 1)
    apart = jnp.abs(row - column)
    apart = jnp.minimum(apart, ny - apart)
    matrix = jnp.zeros((ny, ny), F32)
    for k in range(1, WIDTH + 1):
        matrix = jnp.where(apart == k, H_FACTORS[k - 1] / H_FACTORS[0], matrix)
    matrix = matrix.astype(BF16)
    return jnp.concatenate([matrix, matrix], axis=0)


def along_y(matrix, source, start, count, y_ref, plane_rows):
    step = min(count, WIDTH)
    for i in range(0, count, step):
        block = source[pl.ds((start + i) * plane_rows, step * plane_rows), :]
        parts = jnp.concatenate([block.astype(BF16), low_part(block).astype(BF16)], axis=1)
        y_ref[pl.ds(i * plane_rows, step * plane_rows), :] = jnp.dot(
            parts, matrix, preferred_element_type=F32
        )


def apply_planes(matrix, source, start, count, nx, y_ref, levels, level, linear, emit):
    plane_rows = nx * GROUP
    along_y(matrix, source, start, count, y_ref, plane_rows)
    factors = L_FACTORS if linear else H_FACTORS

    def load(row):
        return source[aligned(row, GROUP), :]

    @pl.loop(0, count)
    def _(i):
        where = (start + i) * plane_rows
        center = [load(where + x * GROUP) for x in range(nx)]
        values = [None] * nx
        half = nx // 2
        for x in range(half):
            shared = {k: center[(x + k) % nx] + center[(x - k) % nx] for k in range(1, half)}
            for at in (x, x + half):
                row = levels[pl.ds((level + i) * nx + at, 1), :]
                row = 0.125 * row + L_CENTER if linear else row + H_CENTER
                total = jnp.broadcast_to(row, center[at].shape) * center[at]
                total = total + factors[0] * y_ref[aligned(i * plane_rows + at * GROUP, GROUP), :]
                for k in range(1, WIDTH + 1):
                    up, down = where + k * plane_rows + at * GROUP, where - k * plane_rows + at * GROUP
                    near = load(up) + load(down) + shared[k if at == x else half - k]
                    total = total + factors[k - 1] * near
                values[at] = total
        emit(i, values, center)


def own_kernel(planes, nx, orbitals_hbm, own_ref, orbitals, semaphores):
    rows = planes * nx
    parts = semaphores.shape[0]
    each = planes // parts
    odd = lax.rem(lax.axis_index("space"), 2)

    def fetch(i):
        at = pl.ds(i * each, each)
        return pltpu.make_async_copy(orbitals_hbm.at[:, at], orbitals.at[:, at], semaphores.at[i])

    for i in range(parts):
        fetch(i).start()
    cells = orbitals.reshape(GROUP * rows, orbitals.shape[-1])
    for i in range(parts):
        fetch(i).wait()

        @pl.loop(i * each, (i + 1) * each)
        def _(plane):
            target = lax.select(odd == 1, planes - 1 - plane, plane) * nx
            for x in range(nx):
                value = cells[pl.ds(plane * nx + x, GROUP, stride=rows), :]
                own_ref[aligned((target + x) * GROUP, GROUP), :] = value


def messages_kernel(planes, nx, own_ref, potential_ref, level_ref, near_ref, far_ref, core_ref):
    plane_rows = nx * GROUP
    side, size = WIDTH * plane_rows, planes * plane_rows
    odd = lax.rem(lax.axis_index("space"), 2)
    for start, ref in ((0, near_ref), (side, far_ref)):
        high = own_ref[pl.ds(start, side), :].astype(BF16)
        ref[pl.ds(0, side), :] = high
        core_ref[pl.ds(start, side), :] = high
    for out_ref, plane, at in ((near_ref, 0, side), (core_ref, planes - 1, size)):
        block = own_ref[pl.ds(plane * plane_rows, plane_rows), :]
        out_ref[pl.ds(at, plane_rows), :] = low_part(block).astype(BF16)
    for plane in range(planes):
        source = lax.select(odd == 1, planes - 1 - plane, plane) * nx
        block = potential_ref[aligned(source, nx), :]
        level_ref[pl.ds(plane * nx, nx), :] = block
        core_ref[pl.ds(size + plane_rows + plane * nx, nx), :] = block.astype(BF16)
        if plane < WIDTH:
            near_ref[pl.ds(side + plane_rows + plane * nx, nx), :] = block.astype(BF16)
        else:
            far_ref[pl.ds(side + (plane - WIDTH) * nx, nx), :] = block.astype(BF16)
        if plane < NEAR:
            at = side + plane_rows + (WIDTH + plane) * nx
            near_ref[pl.ds(at, nx), :] = low_part(block).astype(BF16)
        if plane >= planes - NEAR:
            at = size + plane_rows + (planes + plane - (planes - NEAR)) * nx
            core_ref[pl.ds(at, nx), :] = low_part(block).astype(BF16)


NEAR = 2


def place_planes(message, count, field, where, step, plane_rows):
    for i in range(count):
        block = message[pl.ds(i * plane_rows, plane_rows), :]
        field[pl.ds((where + step * i) * plane_rows, plane_rows), :] = block.astype(F32)


def add_low(message, planes, field, where, plane_rows):
    at = pl.ds(where * plane_rows, plane_rows)
    field[at, :] = field[at, :] + message[pl.ds(planes * plane_rows, plane_rows), :].astype(F32)


def place_levels(message, extra, count, nx, levels, where, near):
    for i in range(count):
        block = message[pl.ds(extra + i * nx, nx), :].astype(F32)
        if near <= i < near + NEAR:
            block = block + message[pl.ds(extra + (count + i - near) * nx, nx), :].astype(F32)
        levels[pl.ds((where - i) * nx, nx), :] = block


def store_planes(nx, *refs):
    def emit(i, values, center):
        for x in range(nx):
            for ref, first in refs:
                ref[aligned(((first + i) * nx + x) * GROUP, GROUP), :] = values[x]

    return emit


def store_second(nx, before, start, *refs):
    def emit(i, values, center):
        for x in range(nx):
            row = (i * nx + x) * GROUP
            value = 2.0 * values[x] - before[aligned(start * nx * GROUP + row, GROUP), :]
            for ref, first in refs:
                ref[aligned(first * nx * GROUP + row, GROUP), :] = value

    return emit


def early_kernel(planes, nx, own_ref, level_ref, core_ref, first_ref, field, levels, y_ref):
    plane_rows = nx * GROUP
    field[pl.ds(0, planes * plane_rows), :] = own_ref[...]
    place_planes(core_ref, planes, field, 2 * planes - 1, -1, plane_rows)
    add_low(core_ref, planes, field, planes, plane_rows)
    levels[pl.ds(0, planes * nx), :] = level_ref[...]
    extra = (planes + 1) * plane_rows
    place_levels(core_ref, extra, planes, nx, levels, 2 * planes - 1, planes - NEAR)
    matrix = circulant(y_ref.shape[1])
    apply_planes(
        matrix, field, WIDTH, 2 * planes - 2 * WIDTH, nx, y_ref, levels, WIDTH, True,
        store_planes(nx, (first_ref, 0)),
    )


def pass_kernel(after_ref, in_ref, out_ref):
    del after_ref
    out_ref[...] = in_ref[pl.ds(0, out_ref.shape[0]), :]


def add_below(nx, below, factors, base, emit):
    @pl.loop(0, nx)
    def _(x):
        low = [below[aligned((j * nx + x) * GROUP, GROUP), :] for j in range(WIDTH)]
        for i in range(WIDTH):
            total = base[aligned((i * nx + x) * GROUP, GROUP), :]
            for j in range(i, WIDTH):
                total = total + factors[WIDTH + i - j - 1] * low[j]
            emit(i, x, total)


def emit_rows(nx, ref):
    def emit(i, x, value):
        ref[aligned((i * nx + x) * GROUP, GROUP), :] = value

    return emit


def emit_pairs(nx, narrow, ref):
    def emit(i, x, value):
        row = i * nx + x
        pair = jnp.concatenate([narrow[aligned(row * GROUP, GROUP), :], value], axis=0)
        ref[aligned(row * 2 * GROUP, 2 * GROUP), :] = pair.astype(BF16)

    return emit


TWICE_L_FACTORS = tuple(2.0 * c for c in L_FACTORS)


def first_ahead_kernel(
    planes, nx, own_ref, level_ref, early_ref, first_part_ref, beyond_part_ref, values, y_ref,
):
    side = WIDTH * nx * GROUP
    matrix = circulant(y_ref.shape[1])
    values[pl.ds(0, side), :] = jnp.zeros((side, values.shape[1]), F32)
    values[pl.ds(side, 2 * side), :] = own_ref[...]
    apply_planes(
        matrix, values, WIDTH, WIDTH, nx, y_ref, level_ref, 0, True,
        store_planes(nx, (first_part_ref, 0)),
    )
    values[pl.ds(side, 2 * side), :] = early_ref[...]
    apply_planes(
        matrix, values, WIDTH, WIDTH, nx, y_ref, level_ref, WIDTH, True,
        store_second(nx, own_ref, WIDTH, (beyond_part_ref, 0)),
    )


def near_kernel(
    nx, near_ref, first_part_ref, beyond_part_ref, near_field_ref, first_ref, beyond_ref, core_ref
):
    plane_rows = nx * GROUP
    place_planes(near_ref, WIDTH, near_field_ref, WIDTH - 1, -1, plane_rows)
    add_low(near_ref, WIDTH, near_field_ref, WIDTH - 1, plane_rows)
    add_below(nx, near_field_ref, L_FACTORS, first_part_ref, emit_rows(nx, first_ref))
    add_below(nx, first_ref, TWICE_L_FACTORS, beyond_part_ref, emit_rows(nx, beyond_ref))
    core_ref[...] = beyond_ref[...].astype(BF16)


def ahead_kernel(
    planes, nx, own_ref, level_ref, near_ref, near_field_ref, early_ref, first_ref,
    first_part_ref, second_part_ref, values, levels, y_ref,
):
    plane_rows = nx * GROUP
    side = WIDTH * plane_rows
    matrix = circulant(y_ref.shape[1])
    values[pl.ds(0, side), :] = jnp.zeros((side, values.shape[1]), F32)
    values[pl.ds(side, side), :] = near_field_ref[...]
    values[pl.ds(2 * side, side), :] = own_ref[pl.ds(0, side), :]
    place_levels(near_ref, side + plane_rows, WIDTH, nx, levels, WIDTH - 1, 0)
    apply_planes(
        matrix, values, WIDTH, WIDTH, nx, y_ref, levels, 0, True, store_planes(nx, (first_part_ref, 0))
    )
    values[pl.ds(side, side), :] = first_ref[...]
    values[pl.ds(2 * side, side), :] = early_ref[pl.ds(0, side), :]
    apply_planes(
        matrix, values, WIDTH, WIDTH, nx, y_ref, level_ref, 0, True,
        store_second(nx, own_ref, 0, (second_part_ref, 0)),
    )


def right_ahead_kernel(nx, level_ref, beyond_ref, beside_ref, after_ref, right_part_ref, values, y_ref):
    del after_ref
    plane_rows = nx * GROUP
    side = WIDTH * plane_rows
    matrix = circulant(y_ref.shape[1])
    values[pl.ds(0, side), :] = jnp.zeros((side, values.shape[1]), F32)
    values[pl.ds(side, side), :] = beyond_ref[...]
    place_planes(beside_ref, WIDTH, values, 3 * WIDTH - 1, -1, plane_rows)
    apply_planes(
        matrix, values, WIDTH, WIDTH, nx, y_ref, level_ref, WIDTH, False,
        store_planes(nx, (right_part_ref, 0)),
    )


def middle_kernel(
    nx, far_ref, first_part_ref, second_part_ref, first_low_ref, second_ref, below
):
    place_planes(far_ref, WIDTH, below, WIDTH - 1, -1, nx * GROUP)
    add_below(nx, below, L_FACTORS, first_part_ref, emit_rows(nx, first_low_ref))
    add_below(nx, first_low_ref, TWICE_L_FACTORS, second_part_ref, emit_rows(nx, second_ref))


def behind_kernel(
    planes, nx, level_ref, near_ref, near_field_ref, far_ref, first_low_ref, first_ref, second_ref,
    beyond_ref, right_part_ref, first_part_ref, second_part_ref, left_part_ref, right_ref, values, levels, y_ref,
):
    plane_rows = nx * GROUP
    side = WIDTH * plane_rows
    add_below(nx, second_ref, H_FACTORS, right_part_ref, emit_pairs(nx, beyond_ref, right_ref))
    matrix = circulant(y_ref.shape[1])
    values[pl.ds(0, side), :] = jnp.zeros((side, values.shape[1]), F32)
    place_levels(far_ref, side, WIDTH, nx, levels, WIDTH - 1, WIDTH)
    place_levels(near_ref, side + plane_rows, WIDTH, nx, levels, 2 * WIDTH - 1, 0)

    place_planes(far_ref, WIDTH, values, 2 * WIDTH - 1, -1, plane_rows)
    values[pl.ds(2 * side, side), :] = near_field_ref[...]
    apply_planes(
        matrix, values, WIDTH, WIDTH, nx, y_ref, levels, 0, True, store_planes(nx, (first_part_ref, 0))
    )
    values[pl.ds(side, side), :] = first_low_ref[...]
    values[pl.ds(2 * side, side), :] = first_ref[...]
    apply_planes(
        matrix, values, WIDTH, WIDTH, nx, y_ref, levels, WIDTH, True,
        store_second(nx, near_field_ref, 0, (second_part_ref, 0)),
    )
    values[pl.ds(side, side), :] = second_ref[...]
    values[pl.ds(2 * side, side), :] = beyond_ref[...]
    apply_planes(
        matrix, values, WIDTH, WIDTH, nx, y_ref, level_ref, 0, False,
        store_planes(nx, (left_part_ref, 0)),
    )


def left_kernel(
    nx, relay_ref, first_part_ref, second_part_ref, left_part_ref, second_ref, beyond_ref, right_ref,
    within_ref, across_ref, below, lower, pairs,
):
    place_planes(relay_ref, WIDTH, below, 0, 1, nx * GROUP)
    add_below(nx, below, L_FACTORS, first_part_ref, emit_rows(nx, lower))
    add_below(nx, lower, TWICE_L_FACTORS, second_part_ref, emit_rows(nx, below))
    add_below(nx, below, H_FACTORS, left_part_ref, emit_pairs(nx, second_ref, pairs))
    me = lax.axis_index("band")
    group = within_ref.shape[0]
    place, upper = lax.rem(me, group), me >= group
    plane = nx * 2 * GROUP
    for j in range(group):
        k = j ^ place
        ref, at = (pairs, 2 * j) if 2 * j < WIDTH else (right_ref, 2 * j - WIDTH)
        within_ref[k, pl.ds(0, 2 * plane), :] = ref[pl.ds(at * plane, 2 * plane), :]
        last = right_ref[pl.ds((2 * group + j - WIDTH) * plane, plane), :]
        within_ref[k, pl.ds(2 * plane, plane), :] = last
        ref, at = (second_ref, 2 * j) if 2 * j < WIDTH else (beyond_ref, 2 * j - WIDTH)

        @pl.when(upper)
        def _():
            across_ref[k] = ref[pl.ds(at * nx * GROUP, plane), :].astype(BF16)

        @pl.when(jnp.logical_not(upper))
        def _():
            across_ref[k] = last


def write_kernel(planes, nx, second_ref, beyond_ref, filtered_ref, done_ref):
    done_ref[...] = jnp.zeros_like(done_ref)
    rows = planes * nx
    odd = lax.rem(lax.axis_index("space"), 2)
    for ref, first in ((second_ref, 0), (beyond_ref, WIDTH)):

        @pl.loop(0, WIDTH)
        def _(i):
            plane = first + i
            target = lax.select(odd == 1, planes - 1 - plane, plane) * nx
            for x in range(nx):
                value = ref[aligned((i * nx + x) * GROUP, GROUP), :]
                filtered_ref[pl.ds(target + x, GROUP, stride=rows), :] = value


def gram_kernel(space, nx, order, *refs):
    after_ref, own_ref, *blocks, out_ref, held = refs
    del after_ref
    band, rows, ny = held.shape
    width = 2 * GROUP
    group = band // 2
    shared, plane = 2 * nx, nx * width
    me = lax.axis_index("band")
    place, upper = lax.rem(me, group), me >= group
    base = me - place
    other = group - base
    held[base + place] = own_ref[...]
    for k, block in zip(order, blocks):
        if k < group:
            held[base + (k ^ place)] = block[...]
            continue
        target = other + ((k - group) ^ place)

        @pl.when(upper)
        def _():
            held[target, pl.ds(0, 2 * plane), :] = jnp.zeros((2 * plane, ny), BF16)
            held[target, pl.ds(2 * plane, plane), :] = block[...]

        @pl.when(jnp.logical_not(upper))
        def _():
            for u in range(nx):
                tile = block[pl.ds(u * width, width), :]
                held[target, pl.ds(2 * u * width, width), :] = tile
                held[target, pl.ds((2 * u + 1) * width, width), :] = tile
            held[target, pl.ds(2 * plane, plane), :] = jnp.zeros((plane, ny), BF16)

    def products(steps):
        total = jnp.zeros((band * width, band * width), F32)
        for i in range(0, len(steps), 2):
            block = jnp.concatenate(
                [held[:, pl.ds(q * width, width), :].reshape(band * width, ny) for q in steps[i : i + 2]],
                axis=1,
            )
            total = total + lax.dot_general(
                block, block, (((1,), (1,)), ((), ())), preferred_element_type=F32
            )
        return total

    even = products(range(0, shared, 2))
    odd = products(range(1, shared, 2))
    total = even + odd + products(range(shared, rows // width))
    lanes = lax.broadcasted_iota(jnp.int32, (GROUP, band * width), 1)
    filtered, lower_lanes = lanes % width < GROUP, lanes < group * width
    crossed = even + pltpu.roll(odd, band * width - GROUP, 1)

    def rows_of(matrix, b):
        return matrix[b * width : b * width + GROUP], matrix[b * width + GROUP : (b + 1) * width]

    def both(matrix, b):
        narrow, applied = rows_of(matrix, b)
        return jnp.where(filtered, narrow, pltpu.roll(applied, GROUP, 1))

    def store(b, piece):
        for s in range(space):
            out_ref[s * band + b] = piece

    zero = jnp.zeros((GROUP, band * width), F32)

    @pl.when(upper)
    def _():
        for b in range(group):
            store(b, jnp.where(lower_lanes, zero, both(total, b)))
            store(group + b, jnp.where(lower_lanes, rows_of(total, group + b)[0], both(total, group + b)))

    @pl.when(jnp.logical_not(upper))
    def _():
        for b in range(group):
            store(b, jnp.where(lower_lanes, both(total, b), both(crossed, b)))
            piece = rows_of(even, group + b)[0] + rows_of(odd, group + b)[1]
            store(group + b, jnp.where(lower_lanes, piece, zero))


def sum_kernel(scale, in_ref, intersection_ref, projected_ref):
    total = in_ref[0]
    for i in range(1, in_ref.shape[0]):
        total = total + in_ref[i]
    total = total * scale
    lanes, columns = total.shape[1], intersection_ref.shape[1]
    source = lax.broadcasted_iota(jnp.int32, (lanes, columns), 0)
    target = lax.broadcasted_iota(jnp.int32, (lanes, columns), 1)
    place = (target // GROUP) * (2 * GROUP) + target % GROUP
    for offset, ref in ((0, intersection_ref), (GROUP, projected_ref)):
        pick = jnp.where(source == place + offset, 1.0, 0.0).astype(F32)
        ref[...] = jnp.dot(total, pick, precision=lax.Precision.HIGHEST, preferred_element_type=F32)


VMEM_FIRST = 53

ORDER = (4, 6, 5, 7, 2, 3, 1)


def call(kernel, outs, *args, scratch=(), hbm_in=0, hbm_out=(), vmem=40, cost=1000000):
    anywhere = pl.BlockSpec(memory_space=pl.ANY)
    return pl.pallas_call(
        kernel,
        out_shape=outs,
        in_specs=[anywhere] * hbm_in + [VMEM] * (len(args) - hbm_in),
        out_specs=tuple(anywhere if i in hbm_out else VMEM for i in range(len(outs))),
        scratch_shapes=list(scratch),
        compiler_params=pltpu.CompilerParams(vmem_limit_bytes=int(vmem * 2**20)),
        cost_estimate=pl.CostEstimate(flops=cost, bytes_accessed=cost, transcendentals=0),
    )(*args)


def shifts(axis):
    count = lax.axis_size(axis)
    up = [(i, (i + 1) % count) for i in range(count)]
    return up, [(j, i) for i, j in up]


def local_kernels(orbitals, potential):
    count, planes, nx, ny = orbitals.shape
    space, band = lax.axis_size("space"), lax.axis_size("band")
    rows = planes * nx
    plane_rows = nx * GROUP
    size = planes * plane_rows
    struct = jax.ShapeDtypeStruct
    other_core = [(i, i ^ 1) for i in range(space)]
    other_chip = [(i, i ^ 3) for i in range(space)]

    def f32_planes(many, height=plane_rows):
        return pltpu.VMEM((many * height, ny), F32)

    def bf16_rows(height):
        return struct((height, ny), BF16)

    half = WIDTH * plane_rows
    slab, half_slab = struct((size, ny), F32), struct((half, ny), F32)
    (own,) = call(
        functools.partial(own_kernel, planes, nx),
        (slab,),
        orbitals,
        hbm_in=1, vmem=VMEM_FIRST,
        scratch=[pltpu.VMEM(orbitals.shape, F32), pltpu.SemaphoreType.DMA((4,))],
    )
    levels, to_near, to_far, to_core = call(
        functools.partial(messages_kernel, planes, nx),
        (
            struct((rows, ny), F32),
            bf16_rows(half + plane_rows + (WIDTH + NEAR) * nx),
            bf16_rows(half + WIDTH * nx),
            bf16_rows(size + plane_rows + (planes + NEAR) * nx),
        ),
        own, potential.reshape(rows, ny),
    )
    near = lax.ppermute(to_near, "space", other_chip)
    core = lax.ppermute(to_core, "space", other_core)
    far = lax.ppermute(to_far, "space", other_chip)
    (early,) = call(
        functools.partial(early_kernel, planes, nx),
        (slab,),
        own, levels, core,
        scratch=[f32_planes(2 * planes), f32_planes(2 * planes, nx), f32_planes(planes)],
    )
    wide = planes + WIDTH
    part = [f32_planes(wide), f32_planes(planes, nx), f32_planes(WIDTH)]
    first_part, beyond_part = call(
        functools.partial(first_ahead_kernel, planes, nx),
        (half_slab,) * 2,
        own, levels, early,
        scratch=[part[0], part[2]],
    )
    near_field, first, beyond, to_beside = call(
        functools.partial(near_kernel, nx),
        (half_slab,) * 3 + (bf16_rows(half),),
        near, first_part, beyond_part,
    )
    beside = lax.ppermute(to_beside, "space", other_core)
    first_part, second_part = call(
        functools.partial(ahead_kernel, planes, nx),
        (half_slab,) * 2,
        own, levels, near, near_field, early, first,
        scratch=part,
    )
    (right_part,) = call(
        functools.partial(right_ahead_kernel, nx),
        (half_slab,),
        levels, beyond, beside, first_part,
        scratch=[part[0], part[2]],
    )
    (relay,) = call(pass_kernel, (bf16_rows(half),), right_part, far, hbm_in=1)
    relay = lax.ppermute(relay, "space", other_core)
    first_low, second = call(
        functools.partial(middle_kernel, nx),
        (half_slab,) * 2,
        far, first_part, second_part,
        scratch=[f32_planes(WIDTH)],
    )
    first_part, second_part, left_part, right = call(
        functools.partial(behind_kernel, planes, nx),
        (half_slab,) * 3 + (bf16_rows(2 * half),),
        levels, near, near_field, far, first_low, first, second, beyond, right_part,
        scratch=part,
    )
    group, plane = band // 2, (nx * 2 * GROUP, ny)
    within, across = call(
        functools.partial(left_kernel, nx),
        (struct((group, 3 * plane[0], ny), BF16), struct((group, *plane), BF16)),
        relay, first_part, second_part, left_part, second, beyond, right,
        scratch=[f32_planes(WIDTH), f32_planes(WIDTH), pltpu.VMEM((2 * half, ny), BF16)],
    )
    filtered, written = call(
        functools.partial(write_kernel, planes, nx),
        (struct((count * rows, ny), F32), struct((GROUP, ny), F32)),
        second, beyond,
        cost=4000000000,
    )
    order = ORDER[::-1]
    blocks = [
        lax.ppermute(
            within[k] if k < group else across[k - group], "band", [(i, i ^ k) for i in range(band)]
        )
        for k in order
    ]
    (pieces,) = call(
        functools.partial(gram_kernel, space, nx, order),
        (struct((space * band, GROUP, band * 2 * GROUP), F32),),
        written, within[0], *blocks,
        hbm_in=1,
        scratch=[pltpu.VMEM((band, 3 * plane[0], ny), BF16)],
    )
    pieces = lax.all_to_all(pieces, ("space", "band"), 0, 0, tiled=True)
    rows_out = struct((count, count * band), F32)
    intersection, projected = call(
        functools.partial(sum_kernel, 1.0 / (rows * ny * space)), (rows_out, rows_out), pieces
    )
    return filtered.reshape(orbitals.shape), intersection, projected


def padded(cells, width):
    up, down = shifts("space")
    head, tail = cells[:, :width], cells[:, cells.shape[1] - width :]
    return jnp.concatenate(
        [lax.ppermute(tail, "space", up), cells, lax.ppermute(head, "space", down)], axis=1
    )


def hamiltonian(beside, potential):
    planes = beside.shape[1] - 2 * WIDTH
    center = beside[:, WIDTH : WIDTH + planes]
    summed = 3.0 * STENCIL[0] * center
    for k in range(1, WIDTH + 1):
        near = beside[:, WIDTH + k : WIDTH + k + planes] + beside[:, WIDTH - k : WIDTH - k + planes]
        for dim in (2, 3):
            near = near + (jnp.roll(center, k, dim) + jnp.roll(center, -k, dim))
        summed = summed + STENCIL[k] * near
    return -0.5 * summed + potential * center


def local_plain(orbitals, potential):
    def step(field):
        return (hamiltonian(padded(field, WIDTH), potential) - 9.0 * field) * 0.125

    filtered = 2.0 * step(step(orbitals)) - orbitals
    beside = padded(filtered.astype(BF16), WIDTH).astype(F32)
    applied = hamiltonian(beside, potential).astype(BF16)
    count = orbitals.shape[0]
    narrow = filtered.astype(BF16).reshape(count, -1)
    applied = applied.reshape(count, -1)
    everyone = lax.all_gather(narrow, "band", axis=0, tiled=True)
    contract = (((1,), (1,)), ((), ()))
    parts = [
        lax.dot_general(rows, everyone, contract, preferred_element_type=F32)
        for rows in (narrow, applied)
    ]
    scale = 1.0 / (narrow.shape[1] * lax.axis_size("space"))
    intersection, projected = lax.psum(tuple(parts), "space")
    return filtered, intersection * scale, projected * scale


def local(orbitals, potential):
    count, planes, nx, ny = orbitals.shape
    band = lax.axis_size("band")
    fits = (
        count == GROUP
        and lax.axis_size("space") == 4
        and planes == 2 * WIDTH
        and nx == 16
        and ny == 128
        and band * 2 * GROUP == 128
        and 2 * planes == 3 * band
    )
    return (local_kernels if fits else local_plain)(orbitals, potential)


def solution(mesh):
    return jax.shard_map(
        local,
        mesh=mesh,
        in_specs=(P("band", "space", None, None), P("space", None, None)),
        out_specs=(P("band", "space", None, None), P("band", None), P("band", None)),
        check_vma=False,
    )
```

```python
import functools

import jax
import jax.numpy as jnp
from jax import lax
from jax.experimental import pallas as pl
from jax.experimental.pallas import tpu as pltpu
from jax.sharding import PartitionSpec as P

STENCIL = (
    -5369.0 / 1800.0,
    12.0 / 7.0,
    -15.0 / 56.0,
    10.0 / 189.0,
    -1.0 / 112.0,
    2.0 / 1925.0,
    -1.0 / 16632.0,
)
WIDTH = 6
BF16 = jnp.bfloat16
F32 = jnp.float32
VMEM = pl.BlockSpec(memory_space=pltpu.VMEM)

GROUP = 8

H_FACTORS = tuple(-0.5 * c for c in STENCIL[1:])
H_CENTER = -1.5 * STENCIL[0]
L_FACTORS = tuple(0.125 * c for c in H_FACTORS)
L_CENTER = (H_CENTER - 9.0) / 8.0


def aligned(start, size):
    return pl.ds(pl.multiple_of(start, size), size)


def low_part(block):
    return block - block.astype(BF16).astype(F32)


def circulant(ny):
    row = lax.broadcasted_iota(jnp.int32, (ny, ny), 0)
    column = lax.broadcasted_iota(jnp.int32, (ny, ny), 1)
    apart = jnp.abs(row - column)
    apart = jnp.minimum(apart, ny - apart)
    matrix = jnp.zeros((ny, ny), F32)
    for k in range(1, WIDTH + 1):
        matrix = jnp.where(apart == k, H_FACTORS[k - 1] / H_FACTORS[0], matrix)
    matrix = matrix.astype(BF16)
    return jnp.concatenate([matrix, matrix], axis=0)


def along_y(matrix, source, start, count, y_ref, plane_rows):
    step = min(count, WIDTH)
    for i in range(0, count, step):
        block = source[pl.ds((start + i) * plane_rows, step * plane_rows), :]
        parts = jnp.concatenate([block.astype(BF16), low_part(block).astype(BF16)], axis=1)
        y_ref[pl.ds(i * plane_rows, step * plane_rows), :] = jnp.dot(
            parts, matrix, preferred_element_type=F32
        )


def apply_planes(matrix, source, start, count, nx, y_ref, levels, level, linear, emit):
    plane_rows = nx * GROUP
    along_y(matrix, source, start, count, y_ref, plane_rows)
    factors = L_FACTORS if linear else H_FACTORS

    def load(row):
        return source[aligned(row, GROUP), :]

    @pl.loop(0, count)
    def _(i):
        where = (start + i) * plane_rows
        center = [load(where + x * GROUP) for x in range(nx)]
        values = [None] * nx
        half = nx // 2
        for x in range(half):
            shared = {k: center[(x + k) % nx] + center[(x - k) % nx] for k in range(1, half)}
            for at in (x, x + half):
                row = levels[pl.ds((level + i) * nx + at, 1), :]
                row = 0.125 * row + L_CENTER if linear else row + H_CENTER
                total = jnp.broadcast_to(row, center[at].shape) * center[at]
                total = total + factors[0] * y_ref[aligned(i * plane_rows + at * GROUP, GROUP), :]
                for k in range(1, WIDTH + 1):
                    up, down = where + k * plane_rows + at * GROUP, where - k * plane_rows + at * GROUP
                    near = load(up) + load(down) + shared[k if at == x else half - k]
                    total = total + factors[k - 1] * near
                values[at] = total
        emit(i, values, center)


def own_kernel(planes, nx, orbitals_hbm, own_ref, orbitals, semaphores):
    rows = planes * nx
    parts = semaphores.shape[0]
    each = planes // parts
    odd = lax.rem(lax.axis_index("space"), 2)

    def fetch(i):
        at = pl.ds(i * each, each)
        return pltpu.make_async_copy(orbitals_hbm.at[:, at], orbitals.at[:, at], semaphores.at[i])

    for i in range(parts):
        fetch(i).start()
    cells = orbitals.reshape(GROUP * rows, orbitals.shape[-1])
    for i in range(parts):
        fetch(i).wait()

        @pl.loop(i * each, (i + 1) * each)
        def _(plane):
            target = lax.select(odd == 1, planes - 1 - plane, plane) * nx
            for x in range(nx):
                value = cells[pl.ds(plane * nx + x, GROUP, stride=rows), :]
                own_ref[aligned((target + x) * GROUP, GROUP), :] = value


def messages_kernel(planes, nx, own_ref, potential_ref, level_ref, near_ref, far_ref, core_ref):
    plane_rows = nx * GROUP
    side, size = WIDTH * plane_rows, planes * plane_rows
    odd = lax.rem(lax.axis_index("space"), 2)
    for start, ref in ((0, near_ref), (side, far_ref)):
        high = own_ref[pl.ds(start, side), :].astype(BF16)
        ref[pl.ds(0, side), :] = high
        core_ref[pl.ds(start, side), :] = high
    for out_ref, plane, at in ((near_ref, 0, side), (core_ref, planes - 1, size)):
        block = own_ref[pl.ds(plane * plane_rows, plane_rows), :]
        out_ref[pl.ds(at, plane_rows), :] = low_part(block).astype(BF16)
    for plane in range(planes):
        source = lax.select(odd == 1, planes - 1 - plane, plane) * nx
        block = potential_ref[aligned(source, nx), :]
        level_ref[pl.ds(plane * nx, nx), :] = block
        core_ref[pl.ds(size + plane_rows + plane * nx, nx), :] = block.astype(BF16)
        if plane < WIDTH:
            near_ref[pl.ds(side + plane_rows + plane * nx, nx), :] = block.astype(BF16)
        else:
            far_ref[pl.ds(side + (plane - WIDTH) * nx, nx), :] = block.astype(BF16)
        if plane < NEAR:
            at = side + plane_rows + (WIDTH + plane) * nx
            near_ref[pl.ds(at, nx), :] = low_part(block).astype(BF16)
        if plane >= planes - NEAR:
            at = size + plane_rows + (planes + plane - (planes - NEAR)) * nx
            core_ref[pl.ds(at, nx), :] = low_part(block).astype(BF16)


NEAR = 2


def place_planes(message, count, field, where, step, plane_rows):
    for i in range(count):
        block = message[pl.ds(i * plane_rows, plane_rows), :]
        field[pl.ds((where + step * i) * plane_rows, plane_rows), :] = block.astype(F32)


def add_low(message, planes, field, where, plane_rows):
    at = pl.ds(where * plane_rows, plane_rows)
    field[at, :] = field[at, :] + message[pl.ds(planes * plane_rows, plane_rows), :].astype(F32)


def place_levels(message, extra, count, nx, levels, where, near):
    for i in range(count):
        block = message[pl.ds(extra + i * nx, nx), :].astype(F32)
        if near <= i < near + NEAR:
            block = block + message[pl.ds(extra + (count + i - near) * nx, nx), :].astype(F32)
        levels[pl.ds((where - i) * nx, nx), :] = block


def store_planes(nx, *refs):
    def emit(i, values, center):
        for x in range(nx):
            for ref, first in refs:
                ref[aligned(((first + i) * nx + x) * GROUP, GROUP), :] = values[x]

    return emit


def store_second(nx, before, start, *refs):
    def emit(i, values, center):
        for x in range(nx):
            row = (i * nx + x) * GROUP
            value = 2.0 * values[x] - before[aligned(start * nx * GROUP + row, GROUP), :]
            for ref, first in refs:
                ref[aligned(first * nx * GROUP + row, GROUP), :] = value

    return emit


def early_kernel(planes, nx, own_ref, level_ref, core_ref, first_ref, field, levels, y_ref):
    plane_rows = nx * GROUP
    field[pl.ds(0, planes * plane_rows), :] = own_ref[...]
    place_planes(core_ref, planes, field, 2 * planes - 1, -1, plane_rows)
    add_low(core_ref, planes, field, planes, plane_rows)
    levels[pl.ds(0, planes * nx), :] = level_ref[...]
    extra = (planes + 1) * plane_rows
    place_levels(core_ref, extra, planes, nx, levels, 2 * planes - 1, planes - NEAR)
    matrix = circulant(y_ref.shape[1])
    apply_planes(
        matrix, field, WIDTH, 2 * planes - 2 * WIDTH, nx, y_ref, levels, WIDTH, True,
        store_planes(nx, (first_ref, 0)),
    )


def pass_kernel(after_ref, in_ref, out_ref):
    del after_ref
    out_ref[...] = in_ref[pl.ds(0, out_ref.shape[0]), :]


def add_below(nx, below, factors, base, emit):
    @pl.loop(0, nx)
    def _(x):
        low = [below[aligned((j * nx + x) * GROUP, GROUP), :] for j in range(WIDTH)]
        for i in range(WIDTH):
            total = base[aligned((i * nx + x) * GROUP, GROUP), :]
            for j in range(i, WIDTH):
                total = total + factors[WIDTH + i - j - 1] * low[j]
            emit(i, x, total)


def emit_rows(nx, ref):
    def emit(i, x, value):
        ref[aligned((i * nx + x) * GROUP, GROUP), :] = value

    return emit


def emit_pairs(nx, narrow, ref):
    def emit(i, x, value):
        row = i * nx + x
        pair = jnp.concatenate([narrow[aligned(row * GROUP, GROUP), :], value], axis=0)
        ref[aligned(row * 2 * GROUP, 2 * GROUP), :] = pair.astype(BF16)

    return emit


TWICE_L_FACTORS = tuple(2.0 * c for c in L_FACTORS)


def first_ahead_kernel(
    planes, nx, own_ref, level_ref, early_ref, first_part_ref, beyond_part_ref, values, y_ref,
):
    side = WIDTH * nx * GROUP
    matrix = circulant(y_ref.shape[1])
    values[pl.ds(0, side), :] = jnp.zeros((side, values.shape[1]), F32)
    values[pl.ds(side, 2 * side), :] = own_ref[...]
    apply_planes(
        matrix, values, WIDTH, WIDTH, nx, y_ref, level_ref, 0, True,
        store_planes(nx, (first_part_ref, 0)),
    )
    values[pl.ds(side, 2 * side), :] = early_ref[...]
    apply_planes(
        matrix, values, WIDTH, WIDTH, nx, y_ref, level_ref, WIDTH, True,
        store_second(nx, own_ref, WIDTH, (beyond_part_ref, 0)),
    )


def near_kernel(
    nx, near_ref, first_part_ref, beyond_part_ref, near_field_ref, first_ref, beyond_ref, core_ref
):
    plane_rows = nx * GROUP
    place_planes(near_ref, WIDTH, near_field_ref, WIDTH - 1, -1, plane_rows)
    add_low(near_ref, WIDTH, near_field_ref, WIDTH - 1, plane_rows)
    add_below(nx, near_field_ref, L_FACTORS, first_part_ref, emit_rows(nx, first_ref))
    add_below(nx, first_ref, TWICE_L_FACTORS, beyond_part_ref, emit_rows(nx, beyond_ref))
    core_ref[...] = beyond_ref[...].astype(BF16)


def ahead_kernel(
    planes, nx, own_ref, level_ref, near_ref, near_field_ref, early_ref, first_ref,
    first_part_ref, second_part_ref, values, levels, y_ref,
):
    plane_rows = nx * GROUP
    side = WIDTH * plane_rows
    matrix = circulant(y_ref.shape[1])
    values[pl.ds(0, side), :] = jnp.zeros((side, values.shape[1]), F32)
    values[pl.ds(side, side), :] = near_field_ref[...]
    values[pl.ds(2 * side, side), :] = own_ref[pl.ds(0, side), :]
    place_levels(near_ref, side + plane_rows, WIDTH, nx, levels, WIDTH - 1, 0)
    apply_planes(
        matrix, values, WIDTH, WIDTH, nx, y_ref, levels, 0, True, store_planes(nx, (first_part_ref, 0))
    )
    values[pl.ds(side, side), :] = first_ref[...]
    values[pl.ds(2 * side, side), :] = early_ref[pl.ds(0, side), :]
    apply_planes(
        matrix, values, WIDTH, WIDTH, nx, y_ref, level_ref, 0, True,
        store_second(nx, own_ref, 0, (second_part_ref, 0)),
    )


def right_ahead_kernel(nx, level_ref, beyond_ref, beside_ref, after_ref, right_part_ref, values, y_ref):
    del after_ref
    plane_rows = nx * GROUP
    side = WIDTH * plane_rows
    matrix = circulant(y_ref.shape[1])
    values[pl.ds(0, side), :] = jnp.zeros((side, values.shape[1]), F32)
    values[pl.ds(side, side), :] = beyond_ref[...]
    place_planes(beside_ref, WIDTH, values, 3 * WIDTH - 1, -1, plane_rows)
    apply_planes(
        matrix, values, WIDTH, WIDTH, nx, y_ref, level_ref, WIDTH, False,
        store_planes(nx, (right_part_ref, 0)),
    )


def middle_kernel(
    nx, far_ref, first_part_ref, second_part_ref, first_low_ref, second_ref, below
):
    place_planes(far_ref, WIDTH, below, WIDTH - 1, -1, nx * GROUP)
    add_below(nx, below, L_FACTORS, first_part_ref, emit_rows(nx, first_low_ref))
    add_below(nx, first_low_ref, TWICE_L_FACTORS, second_part_ref, emit_rows(nx, second_ref))


def behind_kernel(
    planes, nx, level_ref, near_ref, near_field_ref, far_ref, first_low_ref, first_ref, second_ref,
    beyond_ref, right_part_ref, first_part_ref, second_part_ref, left_part_ref, right_ref, values, levels, y_ref,
):
    plane_rows = nx * GROUP
    side = WIDTH * plane_rows
    add_below(nx, second_ref, H_FACTORS, right_part_ref, emit_pairs(nx, beyond_ref, right_ref))
    matrix = circulant(y_ref.shape[1])
    values[pl.ds(0, side), :] = jnp.zeros((side, values.shape[1]), F32)
    place_levels(far_ref, side, WIDTH, nx, levels, WIDTH - 1, WIDTH)
    place_levels(near_ref, side + plane_rows, WIDTH, nx, levels, 2 * WIDTH - 1, 0)

    place_planes(far_ref, WIDTH, values, 2 * WIDTH - 1, -1, plane_rows)
    values[pl.ds(2 * side, side), :] = near_field_ref[...]
    apply_planes(
        matrix, values, WIDTH, WIDTH, nx, y_ref, levels, 0, True, store_planes(nx, (first_part_ref, 0))
    )
    values[pl.ds(side, side), :] = first_low_ref[...]
    values[pl.ds(2 * side, side), :] = first_ref[...]
    apply_planes(
        matrix, values, WIDTH, WIDTH, nx, y_ref, levels, WIDTH, True,
        store_second(nx, near_field_ref, 0, (second_part_ref, 0)),
    )
    values[pl.ds(side, side), :] = second_ref[...]
    values[pl.ds(2 * side, side), :] = beyond_ref[...]
    apply_planes(
        matrix, values, WIDTH, WIDTH, nx, y_ref, level_ref, 0, False,
        store_planes(nx, (left_part_ref, 0)),
    )


def left_kernel(
    nx, relay_ref, first_part_ref, second_part_ref, left_part_ref, second_ref, beyond_ref, right_ref,
    within_ref, across_ref, below, lower, pairs,
):
    place_planes(relay_ref, WIDTH, below, 0, 1, nx * GROUP)
    add_below(nx, below, L_FACTORS, first_part_ref, emit_rows(nx, lower))
    add_below(nx, lower, TWICE_L_FACTORS, second_part_ref, emit_rows(nx, below))
    add_below(nx, below, H_FACTORS, left_part_ref, emit_pairs(nx, second_ref, pairs))
    me = lax.axis_index("band")
    group = within_ref.shape[0]
    place, upper = lax.rem(me, group), me >= group
    plane = nx * 2 * GROUP
    for j in range(group):
        k = j ^ place
        ref, at = (pairs, 2 * j) if 2 * j < WIDTH else (right_ref, 2 * j - WIDTH)
        within_ref[k, pl.ds(0, 2 * plane), :] = ref[pl.ds(at * plane, 2 * plane), :]
        last = right_ref[pl.ds((2 * group + j - WIDTH) * plane, plane), :]
        within_ref[k, pl.ds(2 * plane, plane), :] = last
        ref, at = (second_ref, 2 * j) if 2 * j < WIDTH else (beyond_ref, 2 * j - WIDTH)

        @pl.when(upper)
        def _():
            across_ref[k] = ref[pl.ds(at * nx * GROUP, plane), :].astype(BF16)

        @pl.when(jnp.logical_not(upper))
        def _():
            across_ref[k] = last


def write_kernel(planes, nx, second_ref, beyond_ref, filtered_ref, done_ref):
    done_ref[...] = jnp.zeros_like(done_ref)
    rows = planes * nx
    odd = lax.rem(lax.axis_index("space"), 2)
    for ref, first in ((second_ref, 0), (beyond_ref, WIDTH)):

        @pl.loop(0, WIDTH)
        def _(i):
            plane = first + i
            target = lax.select(odd == 1, planes - 1 - plane, plane) * nx
            for x in range(nx):
                value = ref[aligned((i * nx + x) * GROUP, GROUP), :]
                filtered_ref[pl.ds(target + x, GROUP, stride=rows), :] = value


def gram_kernel(space, nx, order, *refs):
    after_ref, own_ref, *blocks, out_ref, held = refs
    del after_ref
    band, rows, ny = held.shape
    width = 2 * GROUP
    group = band // 2
    shared, plane = 2 * nx, nx * width
    me = lax.axis_index("band")
    place, upper = lax.rem(me, group), me >= group
    base = me - place
    other = group - base
    held[base + place] = own_ref[...]
    for k, block in zip(order, blocks):
        if k < group:
            held[base + (k ^ place)] = block[...]
            continue
        target = other + ((k - group) ^ place)

        @pl.when(upper)
        def _():
            held[target, pl.ds(0, 2 * plane), :] = jnp.zeros((2 * plane, ny), BF16)
            held[target, pl.ds(2 * plane, plane), :] = block[...]

        @pl.when(jnp.logical_not(upper))
        def _():
            for u in range(nx):
                tile = block[pl.ds(u * width, width), :]
                held[target, pl.ds(2 * u * width, width), :] = tile
                held[target, pl.ds((2 * u + 1) * width, width), :] = tile
            held[target, pl.ds(2 * plane, plane), :] = jnp.zeros((plane, ny), BF16)

    def products(steps):
        total = jnp.zeros((band * width, band * width), F32)
        for i in range(0, len(steps), 2):
            block = jnp.concatenate(
                [held[:, pl.ds(q * width, width), :].reshape(band * width, ny) for q in steps[i : i + 2]],
                axis=1,
            )
            total = total + lax.dot_general(
                block, block, (((1,), (1,)), ((), ())), preferred_element_type=F32
            )
        return total

    even = products(range(0, shared, 2))
    odd = products(range(1, shared, 2))
    total = even + odd + products(range(shared, rows // width))
    lanes = lax.broadcasted_iota(jnp.int32, (GROUP, band * width), 1)
    filtered, lower_lanes = lanes % width < GROUP, lanes < group * width
    crossed = even + pltpu.roll(odd, band * width - GROUP, 1)

    def rows_of(matrix, b):
        return matrix[b * width : b * width + GROUP], matrix[b * width + GROUP : (b + 1) * width]

    def both(matrix, b):
        narrow, applied = rows_of(matrix, b)
        return jnp.where(filtered, narrow, pltpu.roll(applied, GROUP, 1))

    def store(b, piece):
        for s in range(space):
            out_ref[s * band + b] = piece

    zero = jnp.zeros((GROUP, band * width), F32)

    @pl.when(upper)
    def _():
        for b in range(group):
            store(b, jnp.where(lower_lanes, zero, both(total, b)))
            store(group + b, jnp.where(lower_lanes, rows_of(total, group + b)[0], both(total, group + b)))

    @pl.when(jnp.logical_not(upper))
    def _():
        for b in range(group):
            store(b, jnp.where(lower_lanes, both(total, b), both(crossed, b)))
            piece = rows_of(even, group + b)[0] + rows_of(odd, group + b)[1]
            store(group + b, jnp.where(lower_lanes, piece, zero))


def sum_kernel(scale, in_ref, intersection_ref, projected_ref):
    total = in_ref[0]
    for i in range(1, in_ref.shape[0]):
        total = total + in_ref[i]
    total = total * scale
    lanes, columns = total.shape[1], intersection_ref.shape[1]
    source = lax.broadcasted_iota(jnp.int32, (lanes, columns), 0)
    target = lax.broadcasted_iota(jnp.int32, (lanes, columns), 1)
    place = (target // GROUP) * (2 * GROUP) + target % GROUP
    for offset, ref in ((0, intersection_ref), (GROUP, projected_ref)):
        pick = jnp.where(source == place + offset, 1.0, 0.0).astype(F32)
        ref[...] = jnp.dot(total, pick, precision=lax.Precision.HIGHEST, preferred_element_type=F32)


VMEM_FIRST = 53

ORDER = (6, 4, 7, 5, 2, 3, 1)


def call(kernel, outs, *args, scratch=(), hbm_in=0, hbm_out=(), vmem=40, cost=1000000):
    anywhere = pl.BlockSpec(memory_space=pl.ANY)
    return pl.pallas_call(
        kernel,
        out_shape=outs,
        in_specs=[anywhere] * hbm_in + [VMEM] * (len(args) - hbm_in),
        out_specs=tuple(anywhere if i in hbm_out else VMEM for i in range(len(outs))),
        scratch_shapes=list(scratch),
        compiler_params=pltpu.CompilerParams(vmem_limit_bytes=int(vmem * 2**20)),
        cost_estimate=pl.CostEstimate(flops=cost, bytes_accessed=cost, transcendentals=0),
    )(*args)


def shifts(axis):
    count = lax.axis_size(axis)
    up = [(i, (i + 1) % count) for i in range(count)]
    return up, [(j, i) for i, j in up]


def local_kernels(orbitals, potential):
    count, planes, nx, ny = orbitals.shape
    space, band = lax.axis_size("space"), lax.axis_size("band")
    rows = planes * nx
    plane_rows = nx * GROUP
    size = planes * plane_rows
    struct = jax.ShapeDtypeStruct
    other_core = [(i, i ^ 1) for i in range(space)]
    other_chip = [(i, i ^ 3) for i in range(space)]

    def f32_planes(many, height=plane_rows):
        return pltpu.VMEM((many * height, ny), F32)

    def bf16_rows(height):
        return struct((height, ny), BF16)

    half = WIDTH * plane_rows
    slab, half_slab = struct((size, ny), F32), struct((half, ny), F32)
    (own,) = call(
        functools.partial(own_kernel, planes, nx),
        (slab,),
        orbitals,
        hbm_in=1, vmem=VMEM_FIRST,
        scratch=[pltpu.VMEM(orbitals.shape, F32), pltpu.SemaphoreType.DMA((4,))],
    )
    levels, to_near, to_far, to_core = call(
        functools.partial(messages_kernel, planes, nx),
        (
            struct((rows, ny), F32),
            bf16_rows(half + plane_rows + (WIDTH + NEAR) * nx),
            bf16_rows(half + WIDTH * nx),
            bf16_rows(size + plane_rows + (planes + NEAR) * nx),
        ),
        own, potential.reshape(rows, ny),
    )
    near = lax.ppermute(to_near, "space", other_chip)
    core = lax.ppermute(to_core, "space", other_core)
    far = lax.ppermute(to_far, "space", other_chip)
    (early,) = call(
        functools.partial(early_kernel, planes, nx),
        (slab,),
        own, levels, core,
        scratch=[f32_planes(2 * planes), f32_planes(2 * planes, nx), f32_planes(planes)],
    )
    wide = planes + WIDTH
    part = [f32_planes(wide), f32_planes(planes, nx), f32_planes(WIDTH)]
    first_part, beyond_part = call(
        functools.partial(first_ahead_kernel, planes, nx),
        (half_slab,) * 2,
        own, levels, early,
        scratch=[part[0], part[2]],
    )
    near_field, first, beyond, to_beside = call(
        functools.partial(near_kernel, nx),
        (half_slab,) * 3 + (bf16_rows(half),),
        near, first_part, beyond_part,
    )
    beside = lax.ppermute(to_beside, "space", other_core)
    first_part, second_part = call(
        functools.partial(ahead_kernel, planes, nx),
        (half_slab,) * 2,
        own, levels, near, near_field, early, first,
        scratch=part,
    )
    (right_part,) = call(
        functools.partial(right_ahead_kernel, nx),
        (half_slab,),
        levels, beyond, beside, first_part,
        scratch=[part[0], part[2]],
    )
    (relay,) = call(pass_kernel, (bf16_rows(half),), right_part, far, hbm_in=1)
    relay = lax.ppermute(relay, "space", other_core)
    first_low, second = call(
        functools.partial(middle_kernel, nx),
        (half_slab,) * 2,
        far, first_part, second_part,
        scratch=[f32_planes(WIDTH)],
    )
    first_part, second_part, left_part, right = call(
        functools.partial(behind_kernel, planes, nx),
        (half_slab,) * 3 + (bf16_rows(2 * half),),
        levels, near, near_field, far, first_low, first, second, beyond, right_part,
        scratch=part,
    )
    group, plane = band // 2, (nx * 2 * GROUP, ny)
    within, across = call(
        functools.partial(left_kernel, nx),
        (struct((group, 3 * plane[0], ny), BF16), struct((group, *plane), BF16)),
        relay, first_part, second_part, left_part, second, beyond, right,
        scratch=[f32_planes(WIDTH), f32_planes(WIDTH), pltpu.VMEM((2 * half, ny), BF16)],
    )
    filtered, written = call(
        functools.partial(write_kernel, planes, nx),
        (struct((count * rows, ny), F32), struct((GROUP, ny), F32)),
        second, beyond,
        cost=4000000000,
    )
    order = ORDER[::-1]
    blocks = [
        lax.ppermute(
            within[k] if k < group else across[k - group], "band", [(i, i ^ k) for i in range(band)]
        )
        for k in order
    ]
    (pieces,) = call(
        functools.partial(gram_kernel, space, nx, order),
        (struct((space * band, GROUP, band * 2 * GROUP), F32),),
        written, within[0], *blocks,
        hbm_in=1,
        scratch=[pltpu.VMEM((band, 3 * plane[0], ny), BF16)],
    )
    pieces = lax.all_to_all(pieces, ("space", "band"), 0, 0, tiled=True)
    rows_out = struct((count, count * band), F32)
    intersection, projected = call(
        functools.partial(sum_kernel, 1.0 / (rows * ny * space)), (rows_out, rows_out), pieces
    )
    return filtered.reshape(orbitals.shape), intersection, projected


def padded(cells, width):
    up, down = shifts("space")
    head, tail = cells[:, :width], cells[:, cells.shape[1] - width :]
    return jnp.concatenate(
        [lax.ppermute(tail, "space", up), cells, lax.ppermute(head, "space", down)], axis=1
    )


def hamiltonian(beside, potential):
    planes = beside.shape[1] - 2 * WIDTH
    center = beside[:, WIDTH : WIDTH + planes]
    summed = 3.0 * STENCIL[0] * center
    for k in range(1, WIDTH + 1):
        near = beside[:, WIDTH + k : WIDTH + k + planes] + beside[:, WIDTH - k : WIDTH - k + planes]
        for dim in (2, 3):
            near = near + (jnp.roll(center, k, dim) + jnp.roll(center, -k, dim))
        summed = summed + STENCIL[k] * near
    return -0.5 * summed + potential * center


def local_plain(orbitals, potential):
    def step(field):
        return (hamiltonian(padded(field, WIDTH), potential) - 9.0 * field) * 0.125

    filtered = 2.0 * step(step(orbitals)) - orbitals
    beside = padded(filtered.astype(BF16), WIDTH).astype(F32)
    applied = hamiltonian(beside, potential).astype(BF16)
    count = orbitals.shape[0]
    narrow = filtered.astype(BF16).reshape(count, -1)
    applied = applied.reshape(count, -1)
    everyone = lax.all_gather(narrow, "band", axis=0, tiled=True)
    contract = (((1,), (1,)), ((), ()))
    parts = [
        lax.dot_general(rows, everyone, contract, preferred_element_type=F32)
        for rows in (narrow, applied)
    ]
    scale = 1.0 / (narrow.shape[1] * lax.axis_size("space"))
    intersection, projected = lax.psum(tuple(parts), "space")
    return filtered, intersection * scale, projected * scale


def local(orbitals, potential):
    count, planes, nx, ny = orbitals.shape
    band = lax.axis_size("band")
    fits = (
        count == GROUP
        and lax.axis_size("space") == 4
        and planes == 2 * WIDTH
        and nx == 16
        and ny == 128
        and band * 2 * GROUP == 128
        and 2 * planes == 3 * band
    )
    return (local_kernels if fits else local_plain)(orbitals, potential)


def solution(mesh):
    return jax.shard_map(
        local,
        mesh=mesh,
        in_specs=(P("band", "space", None, None), P("space", None, None)),
        out_specs=(P("band", "space", None, None), P("band", None), P("band", None)),
        check_vma=False,
    )
```

```python
import functools

import jax
import jax.numpy as jnp
from jax import lax
from jax.experimental import pallas as pl
from jax.experimental.pallas import tpu as pltpu
from jax.sharding import PartitionSpec as P

STENCIL = (
    -5369.0 / 1800.0,
    12.0 / 7.0,
    -15.0 / 56.0,
    10.0 / 189.0,
    -1.0 / 112.0,
    2.0 / 1925.0,
    -1.0 / 16632.0,
)
WIDTH = 6
BF16 = jnp.bfloat16
F32 = jnp.float32
VMEM = pl.BlockSpec(memory_space=pltpu.VMEM)

GROUP = 8

H_FACTORS = tuple(-0.5 * c for c in STENCIL[1:])
H_CENTER = -1.5 * STENCIL[0]
L_FACTORS = tuple(0.125 * c for c in H_FACTORS)
L_CENTER = (H_CENTER - 9.0) / 8.0


def aligned(start, size):
    return pl.ds(pl.multiple_of(start, size), size)


def low_part(block):
    return block - block.astype(BF16).astype(F32)


def circulant(ny):
    row = lax.broadcasted_iota(jnp.int32, (ny, ny), 0)
    column = lax.broadcasted_iota(jnp.int32, (ny, ny), 1)
    apart = jnp.abs(row - column)
    apart = jnp.minimum(apart, ny - apart)
    matrix = jnp.zeros((ny, ny), F32)
    for k in range(1, WIDTH + 1):
        matrix = jnp.where(apart == k, H_FACTORS[k - 1] / H_FACTORS[0], matrix)
    matrix = matrix.astype(BF16)
    return jnp.concatenate([matrix, matrix], axis=0)


def along_y(matrix, source, start, count, y_ref, plane_rows):
    step = min(count, WIDTH)
    for i in range(0, count, step):
        block = source[pl.ds((start + i) * plane_rows, step * plane_rows), :]
        parts = jnp.concatenate([block.astype(BF16), low_part(block).astype(BF16)], axis=1)
        y_ref[pl.ds(i * plane_rows, step * plane_rows), :] = jnp.dot(
            parts, matrix, preferred_element_type=F32
        )


def apply_planes(matrix, source, start, count, nx, y_ref, levels, level, linear, emit):
    plane_rows = nx * GROUP
    along_y(matrix, source, start, count, y_ref, plane_rows)
    factors = L_FACTORS if linear else H_FACTORS

    def load(row):
        return source[aligned(row, GROUP), :]

    @pl.loop(0, count)
    def _(i):
        where = (start + i) * plane_rows
        center = [load(where + x * GROUP) for x in range(nx)]
        values = [None] * nx
        half = nx // 2
        for x in range(half):
            shared = {k: center[(x + k) % nx] + center[(x - k) % nx] for k in range(1, half)}
            for at in (x, x + half):
                row = levels[pl.ds((level + i) * nx + at, 1), :]
                row = 0.125 * row + L_CENTER if linear else row + H_CENTER
                total = jnp.broadcast_to(row, center[at].shape) * center[at]
                total = total + factors[0] * y_ref[aligned(i * plane_rows + at * GROUP, GROUP), :]
                for k in range(1, WIDTH + 1):
                    up, down = where + k * plane_rows + at * GROUP, where - k * plane_rows + at * GROUP
                    near = load(up) + load(down) + shared[k if at == x else half - k]
                    total = total + factors[k - 1] * near
                values[at] = total
        emit(i, values, center)


def own_kernel(planes, nx, orbitals_hbm, own_ref, orbitals, semaphores):
    rows = planes * nx
    parts = semaphores.shape[0]
    each = planes // parts
    odd = lax.rem(lax.axis_index("space"), 2)

    def fetch(i):
        at = pl.ds(i * each, each)
        return pltpu.make_async_copy(orbitals_hbm.at[:, at], orbitals.at[:, at], semaphores.at[i])

    for i in range(parts):
        fetch(i).start()
    cells = orbitals.reshape(GROUP * rows, orbitals.shape[-1])
    for i in range(parts):
        fetch(i).wait()

        @pl.loop(i * each, (i + 1) * each)
        def _(plane):
            target = lax.select(odd == 1, planes - 1 - plane, plane) * nx
            for x in range(nx):
                value = cells[pl.ds(plane * nx + x, GROUP, stride=rows), :]
                own_ref[aligned((target + x) * GROUP, GROUP), :] = value


def messages_kernel(planes, nx, own_ref, potential_ref, level_ref, near_ref, far_ref, core_ref):
    plane_rows = nx * GROUP
    side, size = WIDTH * plane_rows, planes * plane_rows
    odd = lax.rem(lax.axis_index("space"), 2)
    for start, ref in ((0, near_ref), (side, far_ref)):
        high = own_ref[pl.ds(start, side), :].astype(BF16)
        ref[pl.ds(0, side), :] = high
        core_ref[pl.ds(start, side), :] = high
    for out_ref, plane, at in ((near_ref, 0, side), (core_ref, planes - 1, size)):
        block = own_ref[pl.ds(plane * plane_rows, plane_rows), :]
        out_ref[pl.ds(at, plane_rows), :] = low_part(block).astype(BF16)
    for plane in range(planes):
        source = lax.select(odd == 1, planes - 1 - plane, plane) * nx
        block = potential_ref[aligned(source, nx), :]
        level_ref[pl.ds(plane * nx, nx), :] = block
        core_ref[pl.ds(size + plane_rows + plane * nx, nx), :] = block.astype(BF16)
        if plane < WIDTH:
            near_ref[pl.ds(side + plane_rows + plane * nx, nx), :] = block.astype(BF16)
        else:
            far_ref[pl.ds(side + (plane - WIDTH) * nx, nx), :] = block.astype(BF16)
        if plane < NEAR:
            at = side + plane_rows + (WIDTH + plane) * nx
            near_ref[pl.ds(at, nx), :] = low_part(block).astype(BF16)
        if plane >= planes - NEAR:
            at = size + plane_rows + (planes + plane - (planes - NEAR)) * nx
            core_ref[pl.ds(at, nx), :] = low_part(block).astype(BF16)


NEAR = 2


def place_planes(message, count, field, where, step, plane_rows):
    for i in range(count):
        block = message[pl.ds(i * plane_rows, plane_rows), :]
        field[pl.ds((where + step * i) * plane_rows, plane_rows), :] = block.astype(F32)


def add_low(message, planes, field, where, plane_rows):
    at = pl.ds(where * plane_rows, plane_rows)
    field[at, :] = field[at, :] + message[pl.ds(planes * plane_rows, plane_rows), :].astype(F32)


def place_levels(message, extra, count, nx, levels, where, near):
    for i in range(count):
        block = message[pl.ds(extra + i * nx, nx), :].astype(F32)
        if near <= i < near + NEAR:
            block = block + message[pl.ds(extra + (count + i - near) * nx, nx), :].astype(F32)
        levels[pl.ds((where - i) * nx, nx), :] = block


def store_planes(nx, *refs):
    def emit(i, values, center):
        for x in range(nx):
            for ref, first in refs:
                ref[aligned(((first + i) * nx + x) * GROUP, GROUP), :] = values[x]

    return emit


def store_second(nx, before, start, *refs):
    def emit(i, values, center):
        for x in range(nx):
            row = (i * nx + x) * GROUP
            value = 2.0 * values[x] - before[aligned(start * nx * GROUP + row, GROUP), :]
            for ref, first in refs:
                ref[aligned(first * nx * GROUP + row, GROUP), :] = value

    return emit


def early_kernel(planes, nx, own_ref, level_ref, core_ref, first_ref, field, levels, y_ref):
    plane_rows = nx * GROUP
    field[pl.ds(0, planes * plane_rows), :] = own_ref[...]
    place_planes(core_ref, planes, field, 2 * planes - 1, -1, plane_rows)
    add_low(core_ref, planes, field, planes, plane_rows)
    levels[pl.ds(0, planes * nx), :] = level_ref[...]
    extra = (planes + 1) * plane_rows
    place_levels(core_ref, extra, planes, nx, levels, 2 * planes - 1, planes - NEAR)
    matrix = circulant(y_ref.shape[1])
    apply_planes(
        matrix, field, WIDTH, 2 * planes - 2 * WIDTH, nx, y_ref, levels, WIDTH, True,
        store_planes(nx, (first_ref, 0)),
    )


def pass_kernel(after_ref, in_ref, out_ref):
    del after_ref
    out_ref[...] = in_ref[pl.ds(0, out_ref.shape[0]), :]


def add_below(nx, below, factors, base, emit):
    @pl.loop(0, nx)
    def _(x):
        low = [below[aligned((j * nx + x) * GROUP, GROUP), :] for j in range(WIDTH)]
        for i in range(WIDTH):
            total = base[aligned((i * nx + x) * GROUP, GROUP), :]
            for j in range(i, WIDTH):
                total = total + factors[WIDTH + i - j - 1] * low[j]
            emit(i, x, total)


def emit_rows(nx, ref):
    def emit(i, x, value):
        ref[aligned((i * nx + x) * GROUP, GROUP), :] = value

    return emit


def emit_pairs(nx, narrow, ref):
    def emit(i, x, value):
        row = i * nx + x
        pair = jnp.concatenate([narrow[aligned(row * GROUP, GROUP), :], value], axis=0)
        ref[aligned(row * 2 * GROUP, 2 * GROUP), :] = pair.astype(BF16)

    return emit


TWICE_L_FACTORS = tuple(2.0 * c for c in L_FACTORS)


def first_ahead_kernel(
    planes, nx, own_ref, level_ref, early_ref, first_part_ref, beyond_part_ref, values, y_ref,
):
    side = WIDTH * nx * GROUP
    matrix = circulant(y_ref.shape[1])
    values[pl.ds(0, side), :] = jnp.zeros((side, values.shape[1]), F32)
    values[pl.ds(side, 2 * side), :] = own_ref[...]
    apply_planes(
        matrix, values, WIDTH, WIDTH, nx, y_ref, level_ref, 0, True,
        store_planes(nx, (first_part_ref, 0)),
    )
    values[pl.ds(side, 2 * side), :] = early_ref[...]
    apply_planes(
        matrix, values, WIDTH, WIDTH, nx, y_ref, level_ref, WIDTH, True,
        store_second(nx, own_ref, WIDTH, (beyond_part_ref, 0)),
    )


def near_kernel(
    nx, near_ref, first_part_ref, beyond_part_ref, near_field_ref, first_ref, beyond_ref, core_ref
):
    plane_rows = nx * GROUP
    place_planes(near_ref, WIDTH, near_field_ref, WIDTH - 1, -1, plane_rows)
    add_low(near_ref, WIDTH, near_field_ref, WIDTH - 1, plane_rows)
    add_below(nx, near_field_ref, L_FACTORS, first_part_ref, emit_rows(nx, first_ref))
    add_below(nx, first_ref, TWICE_L_FACTORS, beyond_part_ref, emit_rows(nx, beyond_ref))
    core_ref[...] = beyond_ref[...].astype(BF16)


def ahead_kernel(
    planes, nx, own_ref, level_ref, near_ref, near_field_ref, early_ref, first_ref,
    first_part_ref, second_part_ref, values, levels, y_ref,
):
    plane_rows = nx * GROUP
    side = WIDTH * plane_rows
    matrix = circulant(y_ref.shape[1])
    values[pl.ds(0, side), :] = jnp.zeros((side, values.shape[1]), F32)
    values[pl.ds(side, side), :] = near_field_ref[...]
    values[pl.ds(2 * side, side), :] = own_ref[pl.ds(0, side), :]
    place_levels(near_ref, side + plane_rows, WIDTH, nx, levels, WIDTH - 1, 0)
    apply_planes(
        matrix, values, WIDTH, WIDTH, nx, y_ref, levels, 0, True, store_planes(nx, (first_part_ref, 0))
    )
    values[pl.ds(side, side), :] = first_ref[...]
    values[pl.ds(2 * side, side), :] = early_ref[pl.ds(0, side), :]
    apply_planes(
        matrix, values, WIDTH, WIDTH, nx, y_ref, level_ref, 0, True,
        store_second(nx, own_ref, 0, (second_part_ref, 0)),
    )


def right_ahead_kernel(nx, level_ref, beyond_ref, beside_ref, after_ref, right_part_ref, values, y_ref):
    del after_ref
    plane_rows = nx * GROUP
    side = WIDTH * plane_rows
    matrix = circulant(y_ref.shape[1])
    values[pl.ds(0, side), :] = jnp.zeros((side, values.shape[1]), F32)
    values[pl.ds(side, side), :] = beyond_ref[...]
    place_planes(beside_ref, WIDTH, values, 3 * WIDTH - 1, -1, plane_rows)
    apply_planes(
        matrix, values, WIDTH, WIDTH, nx, y_ref, level_ref, WIDTH, False,
        store_planes(nx, (right_part_ref, 0)),
    )


def middle_kernel(
    nx, far_ref, first_part_ref, second_part_ref, first_low_ref, second_ref, below
):
    place_planes(far_ref, WIDTH, below, WIDTH - 1, -1, nx * GROUP)
    add_below(nx, below, L_FACTORS, first_part_ref, emit_rows(nx, first_low_ref))
    add_below(nx, first_low_ref, TWICE_L_FACTORS, second_part_ref, emit_rows(nx, second_ref))


def behind_kernel(
    planes, nx, level_ref, near_ref, near_field_ref, far_ref, first_low_ref, first_ref, second_ref,
    beyond_ref, right_part_ref, first_part_ref, second_part_ref, left_part_ref, right_ref, values, levels, y_ref,
):
    plane_rows = nx * GROUP
    side = WIDTH * plane_rows
    add_below(nx, second_ref, H_FACTORS, right_part_ref, emit_pairs(nx, beyond_ref, right_ref))
    matrix = circulant(y_ref.shape[1])
    values[pl.ds(0, side), :] = jnp.zeros((side, values.shape[1]), F32)
    place_levels(far_ref, side, WIDTH, nx, levels, WIDTH - 1, WIDTH)
    place_levels(near_ref, side + plane_rows, WIDTH, nx, levels, 2 * WIDTH - 1, 0)

    place_planes(far_ref, WIDTH, values, 2 * WIDTH - 1, -1, plane_rows)
    values[pl.ds(2 * side, side), :] = near_field_ref[...]
    apply_planes(
        matrix, values, WIDTH, WIDTH, nx, y_ref, levels, 0, True, store_planes(nx, (first_part_ref, 0))
    )
    values[pl.ds(side, side), :] = first_low_ref[...]
    values[pl.ds(2 * side, side), :] = first_ref[...]
    apply_planes(
        matrix, values, WIDTH, WIDTH, nx, y_ref, levels, WIDTH, True,
        store_second(nx, near_field_ref, 0, (second_part_ref, 0)),
    )
    values[pl.ds(side, side), :] = second_ref[...]
    values[pl.ds(2 * side, side), :] = beyond_ref[...]
    apply_planes(
        matrix, values, WIDTH, WIDTH, nx, y_ref, level_ref, 0, False,
        store_planes(nx, (left_part_ref, 0)),
    )


def left_kernel(
    nx, relay_ref, first_part_ref, second_part_ref, left_part_ref, second_ref, beyond_ref, right_ref,
    within_ref, across_ref, below, lower, pairs,
):
    place_planes(relay_ref, WIDTH, below, 0, 1, nx * GROUP)
    add_below(nx, below, L_FACTORS, first_part_ref, emit_rows(nx, lower))
    add_below(nx, lower, TWICE_L_FACTORS, second_part_ref, emit_rows(nx, below))
    add_below(nx, below, H_FACTORS, left_part_ref, emit_pairs(nx, second_ref, pairs))
    me = lax.axis_index("band")
    group = within_ref.shape[0]
    place, upper = lax.rem(me, group), me >= group
    plane = nx * 2 * GROUP
    for j in range(group):
        k = j ^ place
        ref, at = (pairs, 2 * j) if 2 * j < WIDTH else (right_ref, 2 * j - WIDTH)
        within_ref[k, pl.ds(0, 2 * plane), :] = ref[pl.ds(at * plane, 2 * plane), :]
        last = right_ref[pl.ds((2 * group + j - WIDTH) * plane, plane), :]
        within_ref[k, pl.ds(2 * plane, plane), :] = last
        ref, at = (second_ref, 2 * j) if 2 * j < WIDTH else (beyond_ref, 2 * j - WIDTH)

        @pl.when(upper)
        def _():
            across_ref[k] = ref[pl.ds(at * nx * GROUP, plane), :].astype(BF16)

        @pl.when(jnp.logical_not(upper))
        def _():
            across_ref[k] = last


def write_kernel(planes, nx, second_ref, beyond_ref, filtered_ref, done_ref):
    done_ref[...] = jnp.zeros_like(done_ref)
    rows = planes * nx
    odd = lax.rem(lax.axis_index("space"), 2)
    for ref, first in ((second_ref, 0), (beyond_ref, WIDTH)):

        @pl.loop(0, WIDTH)
        def _(i):
            plane = first + i
            target = lax.select(odd == 1, planes - 1 - plane, plane) * nx
            for x in range(nx):
                value = ref[aligned((i * nx + x) * GROUP, GROUP), :]
                filtered_ref[pl.ds(target + x, GROUP, stride=rows), :] = value


def gram_kernel(space, nx, order, *refs):
    after_ref, own_ref, *blocks, out_ref, held = refs
    del after_ref
    band, rows, ny = held.shape
    width = 2 * GROUP
    group = band // 2
    shared, plane = 2 * nx, nx * width
    me = lax.axis_index("band")
    place, upper = lax.rem(me, group), me >= group
    base = me - place
    other = group - base
    held[base + place] = own_ref[...]
    for k, block in zip(order, blocks):
        if k < group:
            held[base + (k ^ place)] = block[...]
            continue
        target = other + ((k - group) ^ place)

        @pl.when(upper)
        def _():
            held[target, pl.ds(0, 2 * plane), :] = jnp.zeros((2 * plane, ny), BF16)
            held[target, pl.ds(2 * plane, plane), :] = block[...]

        @pl.when(jnp.logical_not(upper))
        def _():
            for u in range(nx):
                tile = block[pl.ds(u * width, width), :]
                held[target, pl.ds(2 * u * width, width), :] = tile
                held[target, pl.ds((2 * u + 1) * width, width), :] = tile
            held[target, pl.ds(2 * plane, plane), :] = jnp.zeros((plane, ny), BF16)

    def products(steps):
        total = jnp.zeros((band * width, band * width), F32)
        for i in range(0, len(steps), 2):
            block = jnp.concatenate(
                [held[:, pl.ds(q * width, width), :].reshape(band * width, ny) for q in steps[i : i + 2]],
                axis=1,
            )
            total = total + lax.dot_general(
                block, block, (((1,), (1,)), ((), ())), preferred_element_type=F32
            )
        return total

    even = products(range(0, shared, 2))
    odd = products(range(1, shared, 2))
    total = even + odd + products(range(shared, rows // width))
    lanes = lax.broadcasted_iota(jnp.int32, (GROUP, band * width), 1)
    filtered, lower_lanes = lanes % width < GROUP, lanes < group * width
    crossed = even + pltpu.roll(odd, band * width - GROUP, 1)

    def rows_of(matrix, b):
        return matrix[b * width : b * width + GROUP], matrix[b * width + GROUP : (b + 1) * width]

    def both(matrix, b):
        narrow, applied = rows_of(matrix, b)
        return jnp.where(filtered, narrow, pltpu.roll(applied, GROUP, 1))

    def store(b, piece):
        for s in range(space):
            out_ref[s * band + b] = piece

    zero = jnp.zeros((GROUP, band * width), F32)

    @pl.when(upper)
    def _():
        for b in range(group):
            store(b, jnp.where(lower_lanes, zero, both(total, b)))
            store(group + b, jnp.where(lower_lanes, rows_of(total, group + b)[0], both(total, group + b)))

    @pl.when(jnp.logical_not(upper))
    def _():
        for b in range(group):
            store(b, jnp.where(lower_lanes, both(total, b), both(crossed, b)))
            piece = rows_of(even, group + b)[0] + rows_of(odd, group + b)[1]
            store(group + b, jnp.where(lower_lanes, piece, zero))


def sum_kernel(scale, in_ref, intersection_ref, projected_ref):
    total = in_ref[0]
    for i in range(1, in_ref.shape[0]):
        total = total + in_ref[i]
    total = total * scale
    lanes, columns = total.shape[1], intersection_ref.shape[1]
    source = lax.broadcasted_iota(jnp.int32, (lanes, 2 * columns), 0)
    target = lax.broadcasted_iota(jnp.int32, (lanes, 2 * columns), 1)
    column = target % columns
    place = (column // GROUP) * (2 * GROUP) + column % GROUP + (target // columns) * GROUP
    pick = jnp.where(source == place, 1.0, 0.0).astype(F32)
    both = jnp.dot(total, pick, precision=lax.Precision.HIGHEST, preferred_element_type=F32)
    intersection_ref[...] = both[:, :columns]
    projected_ref[...] = both[:, columns:]


VMEM_FIRST = 53

ORDER = (6, 4, 7, 5, 2, 3, 1)


def call(kernel, outs, *args, scratch=(), hbm_in=0, hbm_out=(), vmem=40, cost=1000000):
    anywhere = pl.BlockSpec(memory_space=pl.ANY)
    return pl.pallas_call(
        kernel,
        out_shape=outs,
        in_specs=[anywhere] * hbm_in + [VMEM] * (len(args) - hbm_in),
        out_specs=tuple(anywhere if i in hbm_out else VMEM for i in range(len(outs))),
        scratch_shapes=list(scratch),
        compiler_params=pltpu.CompilerParams(vmem_limit_bytes=int(vmem * 2**20)),
        cost_estimate=pl.CostEstimate(flops=cost, bytes_accessed=cost, transcendentals=0),
    )(*args)


def shifts(axis):
    count = lax.axis_size(axis)
    up = [(i, (i + 1) % count) for i in range(count)]
    return up, [(j, i) for i, j in up]


def local_kernels(orbitals, potential):
    count, planes, nx, ny = orbitals.shape
    space, band = lax.axis_size("space"), lax.axis_size("band")
    rows = planes * nx
    plane_rows = nx * GROUP
    size = planes * plane_rows
    struct = jax.ShapeDtypeStruct
    other_core = [(i, i ^ 1) for i in range(space)]
    other_chip = [(i, i ^ 3) for i in range(space)]

    def f32_planes(many, height=plane_rows):
        return pltpu.VMEM((many * height, ny), F32)

    def bf16_rows(height):
        return struct((height, ny), BF16)

    half = WIDTH * plane_rows
    slab, half_slab = struct((size, ny), F32), struct((half, ny), F32)
    (own,) = call(
        functools.partial(own_kernel, planes, nx),
        (slab,),
        orbitals,
        hbm_in=1, vmem=VMEM_FIRST,
        scratch=[pltpu.VMEM(orbitals.shape, F32), pltpu.SemaphoreType.DMA((4,))],
    )
    levels, to_near, to_far, to_core = call(
        functools.partial(messages_kernel, planes, nx),
        (
            struct((rows, ny), F32),
            bf16_rows(half + plane_rows + (WIDTH + NEAR) * nx),
            bf16_rows(half + WIDTH * nx),
            bf16_rows(size + plane_rows + (planes + NEAR) * nx),
        ),
        own, potential.reshape(rows, ny),
    )
    near = lax.ppermute(to_near, "space", other_chip)
    core = lax.ppermute(to_core, "space", other_core)
    far = lax.ppermute(to_far, "space", other_chip)
    (early,) = call(
        functools.partial(early_kernel, planes, nx),
        (slab,),
        own, levels, core,
        scratch=[f32_planes(2 * planes), f32_planes(2 * planes, nx), f32_planes(planes)],
    )
    wide = planes + WIDTH
    part = [f32_planes(wide), f32_planes(planes, nx), f32_planes(WIDTH)]
    first_part, beyond_part = call(
        functools.partial(first_ahead_kernel, planes, nx),
        (half_slab,) * 2,
        own, levels, early,
        scratch=[part[0], part[2]],
    )
    near_field, first, beyond, to_beside = call(
        functools.partial(near_kernel, nx),
        (half_slab,) * 3 + (bf16_rows(half),),
        near, first_part, beyond_part,
    )
    beside = lax.ppermute(to_beside, "space", other_core)
    first_part, second_part = call(
        functools.partial(ahead_kernel, planes, nx),
        (half_slab,) * 2,
        own, levels, near, near_field, early, first,
        scratch=part,
    )
    (right_part,) = call(
        functools.partial(right_ahead_kernel, nx),
        (half_slab,),
        levels, beyond, beside, first_part,
        scratch=[part[0], part[2]],
    )
    (relay,) = call(pass_kernel, (bf16_rows(half),), right_part, far, hbm_in=1)
    relay = lax.ppermute(relay, "space", other_core)
    first_low, second = call(
        functools.partial(middle_kernel, nx),
        (half_slab,) * 2,
        far, first_part, second_part,
        scratch=[f32_planes(WIDTH)],
    )
    first_part, second_part, left_part, right = call(
        functools.partial(behind_kernel, planes, nx),
        (half_slab,) * 3 + (bf16_rows(2 * half),),
        levels, near, near_field, far, first_low, first, second, beyond, right_part,
        scratch=part,
    )
    group, plane = band // 2, (nx * 2 * GROUP, ny)
    within, across = call(
        functools.partial(left_kernel, nx),
        (struct((group, 3 * plane[0], ny), BF16), struct((group, *plane), BF16)),
        relay, first_part, second_part, left_part, second, beyond, right,
        scratch=[f32_planes(WIDTH), f32_planes(WIDTH), pltpu.VMEM((2 * half, ny), BF16)],
    )
    filtered, written = call(
        functools.partial(write_kernel, planes, nx),
        (struct((count * rows, ny), F32), struct((GROUP, ny), F32)),
        second, beyond,
        cost=4000000000,
    )
    order = ORDER[::-1]
    blocks = [
        lax.ppermute(
            within[k] if k < group else across[k - group], "band", [(i, i ^ k) for i in range(band)]
        )
        for k in order
    ]
    (pieces,) = call(
        functools.partial(gram_kernel, space, nx, order),
        (struct((space * band, GROUP, band * 2 * GROUP), F32),),
        written, within[0], *blocks,
        hbm_in=1,
        scratch=[pltpu.VMEM((band, 3 * plane[0], ny), BF16)],
    )
    pieces = lax.all_to_all(pieces, ("space", "band"), 0, 0, tiled=True)
    rows_out = struct((count, count * band), F32)
    intersection, projected = call(
        functools.partial(sum_kernel, 1.0 / (rows * ny * space)), (rows_out, rows_out), pieces
    )
    return filtered.reshape(orbitals.shape), intersection, projected


def padded(cells, width):
    up, down = shifts("space")
    head, tail = cells[:, :width], cells[:, cells.shape[1] - width :]
    return jnp.concatenate(
        [lax.ppermute(tail, "space", up), cells, lax.ppermute(head, "space", down)], axis=1
    )


def hamiltonian(beside, potential):
    planes = beside.shape[1] - 2 * WIDTH
    center = beside[:, WIDTH : WIDTH + planes]
    summed = 3.0 * STENCIL[0] * center
    for k in range(1, WIDTH + 1):
        near = beside[:, WIDTH + k : WIDTH + k + planes] + beside[:, WIDTH - k : WIDTH - k + planes]
        for dim in (2, 3):
            near = near + (jnp.roll(center, k, dim) + jnp.roll(center, -k, dim))
        summed = summed + STENCIL[k] * near
    return -0.5 * summed + potential * center


def local_plain(orbitals, potential):
    def step(field):
        return (hamiltonian(padded(field, WIDTH), potential) - 9.0 * field) * 0.125

    filtered = 2.0 * step(step(orbitals)) - orbitals
    beside = padded(filtered.astype(BF16), WIDTH).astype(F32)
    applied = hamiltonian(beside, potential).astype(BF16)
    count = orbitals.shape[0]
    narrow = filtered.astype(BF16).reshape(count, -1)
    applied = applied.reshape(count, -1)
    everyone = lax.all_gather(narrow, "band", axis=0, tiled=True)
    contract = (((1,), (1,)), ((), ()))
    parts = [
        lax.dot_general(rows, everyone, contract, preferred_element_type=F32)
        for rows in (narrow, applied)
    ]
    scale = 1.0 / (narrow.shape[1] * lax.axis_size("space"))
    intersection, projected = lax.psum(tuple(parts), "space")
    return filtered, intersection * scale, projected * scale


def local(orbitals, potential):
    count, planes, nx, ny = orbitals.shape
    band = lax.axis_size("band")
    fits = (
        count == GROUP
        and lax.axis_size("space") == 4
        and planes == 2 * WIDTH
        and nx == 16
        and ny == 128
        and band * 2 * GROUP == 128
        and 2 * planes == 3 * band
    )
    return (local_kernels if fits else local_plain)(orbitals, potential)


def solution(mesh):
    return jax.shard_map(
        local,
        mesh=mesh,
        in_specs=(P("band", "space", None, None), P("space", None, None)),
        out_specs=(P("band", "space", None, None), P("band", None), P("band", None)),
        check_vma=False,
    )
```
